32 devices in a mesh: group: 2 (over y), seq: 8 (over z, core), mp: 2 (over x).
Axes of the slice: x: 2, y: 2, z: 4, core: 2. Of those that a mesh axis runs over, the one named last changes fastest.
Arguments:
- hidden: bfloat16 [2, 4096, 4096], P('group', 'seq', 'mp'), may hold values from -16 to 16
- w_qkv: bfloat16 [8, 4096, 768], P('mp'), may hold values from -0.09375 to 0.09375
- cache: bfloat16 [1024, 128, 8, 256], P('seq', None, 'mp'), may hold values from -16 to 16
- cache_len: int32 [1024], P('seq'), may hold values from 1 to 128, as said below
- receive: int32 [1024], P('seq'), may hold values 0 or 1
Outputs:
- attended: bfloat16 [2, 4096, 4096], P('group', 'seq', 'mp')
The draws below stay inside these ranges and needn't reach their ends.
Inputs may be any that keep to these rules, and one draw needn't show every extreme that they name: `cache_len`: in each seq shard's 128 requests one has length 128.
All inputs are finite; a program needn't handle non-finite values. No bound on the sum of `receive` on one device may be relied on, other than what follows from the above.
Results may differ from the reference program's by a relative error of at most 0.0098.
Values may be sent and summed in bfloat16 or wider, within the bound.
No kernel may reach another device: no remote copies, remote signals or barrier semaphores. Data moves between devices by JAX's collectives and lax.ppermute only.
A program may use at most 384 MiB of HBM per device.

```python
import jax
import jax.numpy as jnp
from jax import lax

D = 4096
HEADS = 32
KV_HEADS = 8
HEAD_DIM = 128
DRAFT = 4
CACHE = 128
REQ_DEV = 128
ROWS = 4096
BATCH = 1024
QKV_COLS = 768
N_GROUP = 2


def draw_hidden(key, part):
    key = jax.random.fold_in(key, 11)
    base_key = jax.random.fold_in(key, 0)
    array_shape = (N_GROUP, ROWS, D)
    values = jax.random.normal(base_key, array_shape, jnp.float32)
    return jnp.clip(values, -16.0, 16.0).astype(jnp.bfloat16)


def draw_cache(key, part):
    key = jax.random.fold_in(key, 17)
    base_key = jax.random.fold_in(key, 0)
    array_shape = (BATCH, CACHE, KV_HEADS, 2 * HEAD_DIM)
    values = jax.random.normal(base_key, array_shape, jnp.float32)
    return jnp.clip(values, -16.0, 16.0).astype(jnp.bfloat16)


def draw_cache_len(key, part):
    key = jax.random.fold_in(key, 23)
    length_key, chosen_key = jax.random.split(key)
    lengths = jax.random.randint(length_key, (BATCH // REQ_DEV, REQ_DEV), 1, CACHE + 1)
    chosen = jax.random.randint(chosen_key, (BATCH // REQ_DEV, 1), 0, REQ_DEV)
    lengths = jnp.where(jnp.arange(REQ_DEV)[None, :] == chosen, CACHE, lengths)
    return lengths.reshape(BATCH).astype(jnp.int32)


def with_ends(array, rng, smallest, high):
    extent = array.shape
    index_at = [jax.random.randint(jax.random.fold_in(rng, axis), (), 0, extent[axis]) for axis in range(len(extent))]
    array = array.at[tuple(index_at)].set(smallest)
    longest = extent.index(max(extent))
    index_at[longest] = (index_at[longest] + 1) % extent[longest]
    return array.at[tuple(index_at)].set(high)


def block_scale(key, dims, cuts, smallest, high):
    def one(position, blocks):
        heights = jax.random.uniform(jax.random.fold_in(jax.random.fold_in(key, 6), position), (blocks,), jnp.float32, smallest / len(cuts), high / len(cuts))
        return jnp.repeat(jnp.exp(heights), dims[position] // blocks).reshape((-1,) + (1,) * (len(dims) - position - 1))

    factor_of = one(*cuts[0])
    for cut in cuts[1:]:
        factor_of = factor_of * one(*cut)
    return factor_of


def noise(stream_key, shape, scale, most, cuts=(), dtype=jnp.bfloat16):
    factor_of = block_scale(stream_key, shape, cuts, -0.22, 0.18) if cuts else 1.0
    array = jax.random.normal(stream_key, shape, jnp.float32) * scale * factor_of
    return jnp.minimum(jnp.maximum(array, -most), most).astype(dtype)


def setup_inputs(seed: int = 0) -> dict:
    key_list = jax.random.split(jax.random.key(seed), 6)
    return {
        "hidden": draw_hidden(jax.random.fold_in(key_list[5], 71), 0),
        "w_qkv": noise(key_list[1], (KV_HEADS, D, QKV_COLS), D ** -0.5, 0.09375, ((0, 2),)),
        "cache": draw_cache(jax.random.fold_in(key_list[5], 71), 0),
        "cache_len": draw_cache_len(jax.random.fold_in(key_list[5], 71), 0),
        "receive": with_ends((jax.random.randint(key_list[4], (BATCH,), 0, 2) < 1).astype(jnp.int32), jax.random.fold_in(key_list[4], 1), 0, 1),
    }


def widen(values):
    return lax.optimization_barrier(values).astype(jnp.float32)


def project(section_rows, w_qkv):
    return jnp.einsum('rd,gdc->grc', section_rows.astype(jnp.float32), w_qkv.astype(jnp.float32)).astype(jnp.bfloat16)


def split_heads(projected):
    heads_per_group = HEADS // KV_HEADS
    row_count = projected.shape[1]
    queries = projected[:, :, :heads_per_group * HEAD_DIM].reshape(KV_HEADS, row_count, heads_per_group, HEAD_DIM)
    keys = projected[:, :, heads_per_group * HEAD_DIM:(heads_per_group + 1) * HEAD_DIM]
    values = projected[:, :, (heads_per_group + 1) * HEAD_DIM:]
    return queries, keys, values


def prefill_group(operands):
    queries, keys, values = operands
    logits = jnp.einsum('iph,jh->ipj', widen(queries), widen(keys)) * (HEAD_DIM ** -0.5)
    positions = jnp.arange(ROWS)
    allowed = (positions[None, :] <= positions[:, None])[:, None, :]
    logits = jnp.where(allowed, logits, -jnp.inf)
    highest = jnp.max(logits, axis=-1, keepdims=True)
    weights = jnp.exp(logits - highest)
    totals = jnp.sum(weights, axis=-1)
    summed = jnp.einsum('ipj,jh->iph', widen(weights.astype(jnp.bfloat16)), widen(values))
    return (summed / totals[..., None]).astype(jnp.bfloat16)


def reference(hidden, w_qkv, cache, cache_len, receive):
    heads_per_group = HEADS // KV_HEADS
    score_scale = HEAD_DIM ** -0.5
    first_q, first_k, first_v = split_heads(project(hidden[0], w_qkv))
    second_q, second_k, second_v = split_heads(project(hidden[1], w_qkv))
    prefill_out = lax.map(prefill_group, (first_q, first_k, first_v))
    prefill_out = jnp.transpose(prefill_out, (1, 0, 2, 3)).reshape(ROWS, HEADS * HEAD_DIM)
    second_q = second_q.reshape(KV_HEADS, BATCH, DRAFT, heads_per_group, HEAD_DIM)
    second_k = second_k.reshape(KV_HEADS, BATCH, DRAFT, HEAD_DIM)
    second_v = second_v.reshape(KV_HEADS, BATCH, DRAFT, HEAD_DIM)

    def decode_group(operands):
        group_index, queries, own_keys, own_values, prompt_keys, prompt_values = operands
        slab = lax.dynamic_index_in_dim(cache, group_index, 2, False)
        wide_q = widen(queries)
        prompt_logits = jnp.einsum('btph,jh->btpj', wide_q, widen(prompt_keys)) * score_scale
        cache_logits = jnp.einsum('btph,buh->btpu', wide_q, widen(slab[..., :HEAD_DIM])) * score_scale
        own_logits = jnp.einsum('btph,buh->btpu', wide_q, widen(own_keys)) * score_scale
        prompt_ok = (receive > 0)[:, None, None, None]
        cache_ok = (jnp.arange(CACHE)[None, :] < cache_len[:, None])[:, None, None, :]
        own_ok = (jnp.arange(DRAFT)[None, :] <= jnp.arange(DRAFT)[:, None])[None, :, None, :]
        prompt_logits = jnp.where(prompt_ok, prompt_logits, -jnp.inf)
        cache_logits = jnp.where(cache_ok, cache_logits, -jnp.inf)
        own_logits = jnp.where(own_ok, own_logits, -jnp.inf)
        highest = jnp.maximum(jnp.maximum(jnp.max(prompt_logits, axis=-1), jnp.max(cache_logits, axis=-1)), jnp.max(own_logits, axis=-1))[..., None]
        prompt_w = jnp.exp(prompt_logits - highest)
        cache_w = jnp.exp(cache_logits - highest)
        own_w = jnp.exp(own_logits - highest)
        totals = jnp.sum(prompt_w, axis=-1) + jnp.sum(cache_w, axis=-1) + jnp.sum(own_w, axis=-1)
        summed = jnp.einsum('btpj,jh->btph', widen(prompt_w.astype(jnp.bfloat16)), widen(prompt_values))
        summed = summed + jnp.einsum('btpu,buh->btph', widen(cache_w.astype(jnp.bfloat16)), widen(slab[..., HEAD_DIM:]))
        summed = summed + jnp.einsum('btpu,buh->btph', widen(own_w.astype(jnp.bfloat16)), widen(own_values))
        return (summed / totals[..., None]).astype(jnp.bfloat16)

    decode_out = lax.map(decode_group, (jnp.arange(KV_HEADS).astype(jnp.int32), second_q, second_k, second_v, first_k, first_v))
    decode_out = decode_out.reshape(KV_HEADS, ROWS, heads_per_group, HEAD_DIM)
    decode_out = jnp.transpose(decode_out, (1, 0, 2, 3)).reshape(ROWS, HEADS * HEAD_DIM)
    return jnp.stack([prefill_out, decode_out])
```

```python
import functools

import jax
import jax.numpy as jnp
from jax import lax
from jax.experimental import pallas as pl
from jax.experimental.pallas import tpu as pltpu
from jax.sharding import PartitionSpec as P

MASKED_SCORE = -1e30
BLOCK_ROWS = 128
MIB = 1 << 20
NT = (((1,), (1,)), ((), ()))
NN = (((1,), (0,)), ((), ()))


def passed_along(block, axis, distance):
    devices = range(lax.axis_size(axis))
    route = [(i - distance, i) for i in devices if i - distance in devices]
    return lax.ppermute(block, axis, route)


def dot(a, b, dims):
    return lax.dot_general(a, b, dims, preferred_element_type=jnp.float32)


def compiler_params(mib, steps=1):
    return pltpu.CompilerParams(
        dimension_semantics=("arbitrary",) * steps, vmem_limit_bytes=mib * MIB
    )


def kv_kernel(ids, own, own_s, oth, oth_s, wa0, wb0, wa1, wb1, kv0, kv1):
    core = ids[0]
    x_own = jnp.concatenate([own[...], own_s[...]], axis=0)
    x_oth = jnp.concatenate([oth[...], oth_s[...]], axis=0)
    rows = own.shape[0]
    for wa, wb, out in ((wa0, wb0, kv0), (wa1, wb1, kv1)):
        res = (dot(x_own, wa[0], NN) + dot(x_oth, wb[0], NN)).astype(jnp.bfloat16)
        out[core] = res[:rows]
        out[1 - core] = res[rows:]


def project_kv(ids, own, own_s, oth, oth_s, w, chunk, start):
    rows, width = oth.shape
    kv_cols = w.shape[2] // 3
    first = start // rows

    def row_map(i, ids):
        return (first, 0)

    def whole(i, ids):
        return (0, 0)

    def w_map(gi, flip):
        def at(i, ids):
            half = ids[3] if flip == 0 else 1 - ids[3]
            return (2 * ids[0] + gi, half, 2)

        return at

    out_spec = pl.BlockSpec((2, rows, kv_cols), lambda i, ids: (0, 0, 0))
    return pl.pallas_call(
        kv_kernel,
        grid_spec=pltpu.PrefetchScalarGridSpec(
            num_scalar_prefetch=1,
            grid=(1,),
            in_specs=[
                pl.BlockSpec((rows, width), row_map),
                pl.BlockSpec((rows, width), row_map),
                pl.BlockSpec((rows, width), whole),
                pl.BlockSpec((rows, width), whole),
            ]
            + [
                pl.BlockSpec((1, width, kv_cols), w_map(gi, flip))
                for gi in range(2)
                for flip in range(2)
            ],
            out_specs=[out_spec, out_spec],
        ),
        out_shape=[jax.ShapeDtypeStruct((2, rows, kv_cols), jnp.bfloat16)] * 2,
        compiler_params=compiler_params(40),
        cost_estimate=pl.CostEstimate(
            flops=2 * 2 * rows * 2 * width * 2 * kv_cols,
            bytes_accessed=2 * (4 * rows * width + 4 * width * kv_cols),
            transcendentals=0,
        ),
        name="project_kv",
    )(ids, own, own_s, oth, oth_s, w, w, w, w)


def q_kernel(heads, ids, own, own_s, oth, oth_s, wa, wb, kv0, kv1, *refs):
    q_out, theirs = refs[-2:]
    gi = pl.program_id(0)
    core = ids[0]
    rows = own.shape[0]
    x_own = jnp.concatenate([own[...], own_s[...]], axis=0)
    x_oth = jnp.concatenate([oth[...], oth_s[...]], axis=0)
    res = (dot(x_own, wa[0], NN) + dot(x_oth, wb[0], NN)).astype(jnp.bfloat16)
    head_width = res.shape[1] // heads
    per_core = rows // BLOCK_ROWS
    for side in range(2):
        at = core if side == 0 else 1 - core
        for sub in range(per_core):
            for h in range(heads):
                lo = side * rows + sub * BLOCK_ROWS
                q_out[0, at * per_core + sub, h * BLOCK_ROWS : (h + 1) * BLOCK_ROWS, :] = res[
                    lo : lo + BLOCK_ROWS, h * head_width : (h + 1) * head_width
                ]
    theirs[0, :, : heads * head_width] = res[rows:]

    @pl.when(gi == 0)
    def _():
        theirs[0, :, heads * head_width :] = kv0[1 - core]

    @pl.when(gi == 1)
    def _():
        theirs[0, :, heads * head_width :] = kv1[1 - core]


def project_q(ids, own, own_s, oth, oth_s, w, kv0, kv1, before, chunk, start, blocks):
    rows, width = oth.shape
    columns = w.shape[2]
    q_cols = columns * 2 // 3
    kv_cols = columns - q_cols
    heads = q_cols * 2 // kv_cols
    head_width = q_cols // heads
    first = start // rows
    here = 2 * rows // BLOCK_ROWS
    first_block = 2 * start // BLOCK_ROWS // here

    def row_map(i, ids):
        return (first, 0)

    def whole(i, ids):
        return (0, 0)

    def w_map(flip):
        def at(i, ids):
            return (2 * ids[0] + i, ids[3] if flip == 0 else 1 - ids[3], 0)

        return at

    in_specs = (
        [
            pl.BlockSpec((rows, width), row_map),
            pl.BlockSpec((rows, width), row_map),
            pl.BlockSpec((rows, width), whole),
            pl.BlockSpec((rows, width), whole),
        ]
        + [pl.BlockSpec((1, width, q_cols), w_map(flip)) for flip in range(2)]
        + [pl.BlockSpec((2, rows, kv_cols), lambda i, ids: (0, 0, 0))] * 2
    )
    args = [ids, own, own_s, oth, oth_s, w, w, kv0, kv1]
    aliases = {}
    if before is not None:
        in_specs.append(pl.BlockSpec(memory_space=pl.ANY))
        aliases = {len(args): 0}
        args.append(before)
    return pl.pallas_call(
        functools.partial(q_kernel, heads),
        grid_spec=pltpu.PrefetchScalarGridSpec(
            num_scalar_prefetch=1,
            grid=(2,),
            in_specs=in_specs,
            out_specs=[
                pl.BlockSpec(
                    (1, here, heads * BLOCK_ROWS, head_width),
                    lambda i, ids: (i, first_block, 0, 0),
                ),
                pl.BlockSpec((1, rows, columns), lambda i, ids: (i, 0, 0)),
            ],
        ),
        out_shape=[
            jax.ShapeDtypeStruct((2, blocks, heads * BLOCK_ROWS, head_width), jnp.bfloat16),
            jax.ShapeDtypeStruct((2, rows, columns), jnp.bfloat16),
        ],
        input_output_aliases=aliases,
        compiler_params=compiler_params(56),
        cost_estimate=pl.CostEstimate(
            flops=2 * 2 * rows * 2 * width * 2 * q_cols,
            bytes_accessed=2 * (4 * rows * width + 4 * width * q_cols),
            transcendentals=0,
        ),
        name="project_q",
    )(*args)


SUB_REQ = 4


def cache_kernel(heads, draft, step_req, start_req, scale, ids, lens, cache, q, kv0, kv1, swapped, flags, mine, theirs):
    groups, _, slots, both = cache.shape
    width = both // 2
    core = ids[0]
    step = pl.program_id(0)
    rows = SUB_REQ * draft
    per_block = BLOCK_ROWS // (step_req * draft)

    @pl.when(ids[2] == 1)
    def _():
        r_of_row = (lax.broadcasted_iota(jnp.int32, (heads * rows, SUB_REQ * slots), 0) % rows) // draft
        key = lax.broadcasted_iota(jnp.int32, (heads * rows, SUB_REQ * slots), 1)
        r_of_key = key // slots
        slot = key % slots
        own_row = lax.broadcasted_iota(jnp.int32, (heads * rows, rows), 0) % rows
        own_key = lax.broadcasted_iota(jnp.int32, (heads * rows, rows), 1)
        own_ok = (own_row // draft == own_key // draft) & (own_key <= own_row)
        for sub in range(step_req // SUB_REQ):
            req0 = start_req + step * step_req + sub * SUB_REQ
            limit = jnp.zeros((heads * rows, SUB_REQ * slots), jnp.int32)
            for r in range(SUB_REQ):
                limit = jnp.where(r_of_key == r, lens[req0 + r], limit)
            ok = (r_of_row == r_of_key) & (slot < limit)
            row0 = step % per_block * (step_req * draft) + sub * rows
            row0 = pl.multiple_of(row0, rows)
            flat0 = pl.multiple_of(sub * rows, rows)
            for g in range(groups):
                gi = g % 2
                for side in range(2):
                    if g // 2 != side:
                        continue
                    cache_g = 2 * (core if side == 0 else 1 - core) + gi
                    kv = cache[cache_g, sub * SUB_REQ : (sub + 1) * SUB_REQ].reshape(
                        SUB_REQ * slots, both
                    )
                    if side == 0:
                        qs = jnp.concatenate(
                            [
                                q[gi, 0, pl.ds(h * BLOCK_ROWS + row0, rows), :]
                                for h in range(heads)
                            ],
                            axis=0,
                        )
                        own = (kv0 if gi == 0 else kv1)[0, pl.ds(flat0, rows), :]
                    else:
                        block = swapped[gi, pl.ds(flat0, rows), :]
                        qs = jnp.concatenate(
                            [block[:, h * width : (h + 1) * width] for h in range(heads)], axis=0
                        )
                        own = block[:, heads * width :]
                    s = dot(qs, kv[:, :width], NT) * scale
                    s_own = dot(qs, own[:, :width], NT) * scale
                    s = jnp.where(ok, s, MASKED_SCORE)
                    s_own = jnp.where(own_ok, s_own, MASKED_SCORE)
                    top = jnp.maximum(
                        jnp.max(s, axis=1, keepdims=True), jnp.max(s_own, axis=1, keepdims=True)
                    )
                    p = jnp.exp(s - top)
                    p_own = jnp.exp(s_own - top)
                    total = jnp.sum(p, axis=1, keepdims=True) + jnp.sum(
                        p_own, axis=1, keepdims=True
                    )
                    o = dot(p.astype(jnp.bfloat16), kv[:, width:], NN) + dot(
                        p_own.astype(jnp.bfloat16), own[:, width:], NN
                    )
                    o = o / total
                    lse = top + jnp.log(total)
                    out = mine if side == 0 else theirs
                    for h in range(heads):
                        out[gi, sub * rows : (sub + 1) * rows, h * width : (h + 1) * width] = o[
                            h * rows : (h + 1) * rows
                        ]
                        out[
                            gi,
                            sub * rows : (sub + 1) * rows,
                            (heads + h) * width : (heads + h + 1) * width,
                        ] = jnp.broadcast_to(lse[h * rows : (h + 1) * rows], (rows, width)) if False else jnp.broadcast_to(
                            lse[h * rows : (h + 1) * rows], (rows, width)
                        )


def cache_attention(ids, lens, cache_t, q, kv0, kv1, swapped, start, rows, draft, scale):
    groups, _, slots, both = cache_t.shape
    width = both // 2
    heads = q.shape[2] // BLOCK_ROWS
    step_req = 8
    steps = rows // (step_req * draft)
    step_rows = step_req * draft
    start_req = start // draft
    per_block = BLOCK_ROWS // step_rows
    blocks_core = rows // BLOCK_ROWS
    block0 = 2 * start // BLOCK_ROWS

    def q_map(i, ids, lens):
        return (0, block0 + ids[0] * blocks_core + i // per_block, 0, 0)

    out_spec = pl.BlockSpec((2, step_rows, 2 * heads * width), lambda i, ids, lens: (0, i, 0))
    return pl.pallas_call(
        functools.partial(cache_kernel, heads, draft, step_req, start_req, scale),
        grid_spec=pltpu.PrefetchScalarGridSpec(
            num_scalar_prefetch=2,
            grid=(steps,),
            in_specs=[
                pl.BlockSpec(
                    (groups, step_req, slots, both),
                    lambda i, ids, lens: (0, (start_req // step_req + i) * ids[2], 0, 0),
                ),
                pl.BlockSpec((2, 1, heads * BLOCK_ROWS, width), q_map),
                pl.BlockSpec((1, step_rows, both), lambda i, ids, lens: (ids[0], i, 0)),
                pl.BlockSpec((1, step_rows, both), lambda i, ids, lens: (ids[0], i, 0)),
                pl.BlockSpec((2, step_rows, swapped.shape[2]), lambda i, ids, lens: (0, i, 0)),
                pl.BlockSpec(memory_space=pl.ANY),
            ],
            out_specs=[out_spec, out_spec],
        ),
        out_shape=[jax.ShapeDtypeStruct((2, rows, 2 * heads * width), jnp.float32)] * 2,
        compiler_params=compiler_params(40),
        cost_estimate=pl.CostEstimate(
            flops=4 * rows * heads * groups * SUB_REQ * slots * width,
            bytes_accessed=2 * groups * rows // draft * slots * both,
            transcendentals=rows * heads * groups * slots * SUB_REQ,
        ),
        name="cache_attention",
    )(ids, lens, cache_t, q, kv0, kv1, swapped, ids)


def prompt_kernel(
    first, last, slots_n, starts, key_start, rows_core, scale, n_state, ids, *refs
):
    refs = list(refs)
    q = refs.pop(0)
    own = [refs.pop(0), refs.pop(0)]
    arrived = [refs.pop(0) for _ in range(slots_n)]
    if not first:
        acc_in, ml_in = refs.pop(0), refs.pop(0)
    if last:
        part_mine, part_theirs, flags = refs.pop(0), refs.pop(0), refs.pop(0)
        out_ref = refs.pop(0)
    else:
        acc_out, ml_out = refs.pop(0), refs.pop(0)
    kvbuf, acc, m_ref, l_ref, sems = refs
    gi, blk = pl.program_id(0), pl.program_id(1)
    core, z, grp = ids[0], ids[1], ids[2]
    chips = slots_n // 2
    place = jnp.where(grp == 0, z, slots_n - 1 - z)
    keys = kvbuf.shape[2]
    heads = q.shape[2] // BLOCK_ROWS
    width = q.shape[3]

    def copies():
        made = []
        for t in range(slots_n):
            r = lax.rem(place - t + slots_n, slots_n)
            lane = r // chips
            chip = jnp.where(lane == 0, r, slots_n - 1 - r)
            made.append(
                pltpu.make_async_copy(arrived[t], kvbuf.at[lane, chip], sems.at[t])
            )
        return made

    @pl.when((gi == 0) & (blk == 0))
    def _():
        for copy in copies():
            copy.start()
        for copy in copies():
            copy.wait()

    if first:
        acc[...] = jnp.zeros_like(acc)
        m_ref[...] = jnp.full_like(m_ref, MASKED_SCORE)
        l_ref[...] = jnp.zeros_like(l_ref)
    else:
        acc[...] = acc_in[0, 0]
        for h in range(heads):
            m_ref[h * BLOCK_ROWS : (h + 1) * BLOCK_ROWS, :] = jnp.broadcast_to(
                ml_in[0, 0, :, h : h + 1], (BLOCK_ROWS, 128)
            )
            l_ref[h * BLOCK_ROWS : (h + 1) * BLOCK_ROWS, :] = jnp.broadcast_to(
                ml_in[0, 0, :, heads + h : heads + h + 1], (BLOCK_ROWS, 128)
            )

    def visit(k, v, mask):
        s = dot(q[0, 0], k, NT)
        if mask is not None:
            s = jnp.where(mask, s, MASKED_SCORE)
        old = m_ref[:, :1]
        new = jnp.maximum(old, jnp.max(s, axis=1, keepdims=True))
        p = jnp.exp((s - new) * scale)
        fade = jnp.exp((old - new) * scale)
        l_ref[...] = jnp.broadcast_to(
            l_ref[:, :1] * fade + jnp.sum(p, axis=1, keepdims=True), l_ref.shape
        )
        acc[...] = acc[...] * fade + dot(p.astype(jnp.bfloat16), v, NN)
        m_ref[...] = jnp.broadcast_to(new, m_ref.shape)

    def full(chip, carry):
        visit(kvbuf[gi, chip, :, :width], kvbuf[gi, chip, :, width:], None)
        return carry

    lax.fori_loop(0, jnp.where(grp == 0, z, chips), full, 0)

    pos = ids[8 + blk]
    own_rows = own[0].shape[1]
    for kc in range(2):
        key0 = kc * rows_core + key_start

        @pl.when((grp == 0) & (key0 <= pos + BLOCK_ROWS - 1))
        def _():
            shape = (heads * BLOCK_ROWS, own_rows)
            row_pos = pos + lax.broadcasted_iota(jnp.int32, shape, 0) % BLOCK_ROWS
            key_pos = key0 + lax.broadcasted_iota(jnp.int32, shape, 1)
            kv = jnp.where(gi == 0, own[0][kc], own[1][kc])
            visit(kv[:, :width], kv[:, width:], key_pos <= row_pos)

    if not last:
        acc_out[0, 0] = acc[...]
        for h in range(heads):
            ml_out[0, 0, :, h : h + 1] = m_ref[h * BLOCK_ROWS : (h + 1) * BLOCK_ROWS, :1]
            ml_out[0, 0, :, heads + h : heads + h + 1] = l_ref[
                h * BLOCK_ROWS : (h + 1) * BLOCK_ROWS, :1
            ]
    else:

        @pl.when(grp == 0)
        def _():
            o = acc[...] / l_ref[:, :1]
            for h in range(heads):
                out_ref[:, h * width : (h + 1) * width] = o[
                    h * BLOCK_ROWS : (h + 1) * BLOCK_ROWS
                ].astype(jnp.bfloat16)

        @pl.when(grp == 1)
        def _():
            here = pos // rows_core == core
            for h in range(heads):
                part = slice(h * BLOCK_ROWS, (h + 1) * BLOCK_ROWS)
                columns = slice(h * width, (h + 1) * width)
                wide = slice((heads + h) * width, (heads + h + 1) * width)
                o_c = jnp.where(here, part_mine[0, :, columns], part_theirs[0, :, columns])
                lse_c = jnp.where(here, part_mine[0, :, wide], part_theirs[0, :, wide])
                o_p = acc[part] / l_ref[part]
                lse_p = m_ref[part] * scale + jnp.log(l_ref[part])
                lse_p = jnp.where(flags[0] > 0, lse_p, MASKED_SCORE)
                top = jnp.maximum(lse_p, lse_c)
                w_p = jnp.exp(lse_p - top)
                w_c = jnp.exp(lse_c - top)
                out_ref[:, columns] = ((o_p * w_p + o_c * w_c) / (w_p + w_c)).astype(jnp.bfloat16)


def prompt_attention(ids, q, own, arrived, state, merge, starts, sizes, chunk, rows_core, scale):
    slots_n = len(arrived)
    _, blocks, stacked, width = q.shape
    heads = stacked // BLOCK_ROWS
    first, last = state is None, merge is not None
    size = sizes[chunk]
    keys = 2 * size

    def by_block(gi, blk, ids):
        return (gi, blk, 0, 0)

    acc_spec = pl.BlockSpec((1, 1, stacked, width), by_block)
    ml_spec = pl.BlockSpec((1, 1, BLOCK_ROWS, 128), by_block)
    own_spec = pl.BlockSpec((2, size, 2 * width), lambda gi, blk, ids: (0, 0, 0))
    in_specs = [acc_spec, own_spec, own_spec] + [pl.BlockSpec(memory_space=pl.ANY)] * slots_n
    args = [ids, q, *own, *[a.reshape(keys, 2 * width) for a in arrived]]
    if not first:
        in_specs += [acc_spec, ml_spec]
        args += list(state)
    if last:
        def part_map(gi, blk, ids):
            return (gi, ids[8 + blk] % rows_core // BLOCK_ROWS, 0)

        part_spec = pl.BlockSpec((1, BLOCK_ROWS, 2 * heads * width), part_map)
        in_specs += [
            part_spec,
            part_spec,
            pl.BlockSpec((1, BLOCK_ROWS, 128), lambda gi, blk, ids: (blk, 0, 0)),
        ]
        args += list(merge)
        out_specs = [
            pl.BlockSpec(
                (BLOCK_ROWS, heads * width),
                lambda gi, blk, ids: (ids[8 + blk] // BLOCK_ROWS, gi),
            )
        ]
        out_shape = [jax.ShapeDtypeStruct((2 * rows_core, 2 * heads * width), jnp.bfloat16)]
    else:
        out_specs = [acc_spec, ml_spec]
        out_shape = [
            jax.ShapeDtypeStruct((2, blocks, stacked, width), jnp.float32),
            jax.ShapeDtypeStruct((2, blocks, BLOCK_ROWS, 128), jnp.float32),
        ]
    chips = slots_n // 2
    pairs = 2 * blocks * stacked * keys * chips
    return pl.pallas_call(
        functools.partial(
            prompt_kernel,
            first,
            last,
            slots_n,
            starts,
            starts[chunk],
            rows_core,
            scale,
            None,
        ),
        grid_spec=pltpu.PrefetchScalarGridSpec(
            num_scalar_prefetch=1,
            grid=(2, blocks),
            in_specs=in_specs,
            out_specs=out_specs,
            scratch_shapes=[
                pltpu.VMEM((2, chips, keys, 2 * width), jnp.bfloat16),
                pltpu.VMEM((stacked, width), jnp.float32),
                pltpu.VMEM((stacked, 128), jnp.float32),
                pltpu.VMEM((stacked, 128), jnp.float32),
                pltpu.SemaphoreType.DMA((slots_n,)),
            ],
        ),
        out_shape=out_shape,
        compiler_params=compiler_params(48, 2),
        cost_estimate=pl.CostEstimate(
            flops=4 * pairs * width, bytes_accessed=16 * MIB, transcendentals=pairs
        ),
        name="prompt_attention",
    )(*args)


CHUNKS = 2


def fast_shards(hidden, w_qkv, cache, cache_len, receive):
    head_width = cache.shape[3] // 2
    heads = w_qkv.shape[2] // head_width - 2
    rows_core = hidden.shape[1]
    requests = cache.shape[0]
    draft = rows_core // requests
    scale = head_width ** (-0.5)
    seq_n = lax.axis_size("seq")
    chips = seq_n // 2
    ring_n = 2 * chips
    sizes = [rows_core // CHUNKS] * CHUNKS
    starts = [sum(sizes[:c]) for c in range(CHUNKS)]
    blocks = 2 * rows_core // BLOCK_ROWS

    seq_i, group_i, mp_i = lax.axis_index("seq"), lax.axis_index("group"), lax.axis_index("mp")
    core, chip = seq_i % 2, seq_i // 2
    places = []
    for size, start in zip(sizes, starts):
        for c in range(2):
            places += [c * rows_core + start + s for s in range(0, size, BLOCK_ROWS)]
    ids = jnp.concatenate(
        [
            jnp.stack([core, chip, group_i, mp_i]).astype(jnp.int32),
            jnp.zeros((4,), jnp.int32),
            jnp.array(places, jnp.int32),
        ]
    )
    prefill = group_i == 0

    mp_swap = [(0, 1), (1, 0)]
    core_swap = [(i, i ^ 1) for i in range(seq_n)]
    ring = [(0, k) for k in range(chips)] + [(1, chips - 1 - k) for k in range(chips)]
    index = [[g * seq_n + 2 * k + c for c in range(2)] for g, k in ring]
    up = [(index[r][c], index[(r + 1) % ring_n][c]) for r in range(ring_n) for c in range(2)]
    down = [(index[r][c], index[r - 1][c]) for r in range(ring_n) for c in range(2)]

    def swap_cores(x):
        return lax.ppermute(x, "seq", core_swap)

    own = hidden[0]
    oth = [lax.ppermute(own[s : s + n], "mp", mp_swap) for s, n in zip(starts, sizes)]
    own_s = swap_cores(own)
    oth_s = [swap_cores(x) for x in oth]
    flag_mine = jnp.repeat(receive, draft).astype(jnp.float32)
    flag_theirs = swap_cores(flag_mine)
    cache_t = jnp.transpose(cache, (2, 0, 1, 3))

    kvs, arrived, parts = [], [], []
    q = None
    for c, (start, size) in enumerate(zip(starts, sizes)):
        kv0, kv1 = project_kv(ids, own, own_s, oth[c], oth_s[c], w_qkv, c, start)
        crossed = lax.ppermute(kv1, "group", [(0, 1)])
        block = jnp.where(prefill, kv0, crossed)
        ups, downs = [block], [block]
        for step in range(ring_n // 2):
            ups.append(lax.ppermute(ups[-1], ("group", "seq"), up))
            if step < ring_n // 2 - 1:
                downs.append(lax.ppermute(downs[-1], ("group", "seq"), down))
        kvs.append((kv0, kv1))
        arrived.append(ups + downs[:0:-1])
        q, theirs = project_q(
            ids, own, own_s, oth[c], oth_s[c], w_qkv, kv0, kv1, q, c, start, blocks
        )
        swapped = swap_cores(theirs)
        mine, away = cache_attention(
            ids, cache_len, cache_t, q, kv0, kv1, swapped, start, size, draft, scale
        )
        parts.append((mine, swap_cores(away)))
    merge_mine = jnp.concatenate([p[0] for p in parts], axis=1)
    merge_theirs = jnp.concatenate([p[1] for p in parts], axis=1)
    flags_by_core = jnp.where(
        core == 0, jnp.stack([flag_mine, flag_theirs]), jnp.stack([flag_theirs, flag_mine])
    ).reshape(2 * rows_core)
    flags = jnp.stack([flags_by_core[p : p + BLOCK_ROWS] for p in places])
    flags = jnp.broadcast_to(flags[:, :, None], (blocks, BLOCK_ROWS, 128))

    state = None
    for c in range(CHUNKS):
        merge = (merge_mine, merge_theirs, flags) if c == CHUNKS - 1 else None
        state = prompt_attention(
            ids, q, kvs[c], arrived[c], state, merge, starts, sizes, c, rows_core, scale
        )
    done = state[0].reshape(2, rows_core, state[0].shape[1])
    mine = jnp.where(core == 0, done[0], done[1])
    back = swap_cores(jnp.where(core == 0, done[1], done[0]))
    return jnp.where(
        core == 0,
        jnp.concatenate([mine, back], axis=1),
        jnp.concatenate([back, mine], axis=1),
    )[None]


def plain_shards(hidden, w_qkv, cache, cache_len, receive):
    group_count = w_qkv.shape[0]
    column_count = w_qkv.shape[2]
    head_width = cache.shape[3] // 2
    heads_per_group = column_count // head_width - 2
    row_count = hidden.shape[1]
    requests = cache.shape[0]
    draft_count = row_count // requests
    slot_count = cache.shape[1]
    score_scale = head_width ** (-0.5)
    projected = jnp.einsum(
        "rd,gdc->grc",
        lax.all_gather(hidden, "mp", axis=2, tiled=True)[0],
        w_qkv,
        preferred_element_type=jnp.float32,
    ).astype(jnp.bfloat16)
    queries = projected[:, :, : heads_per_group * head_width].reshape(
        group_count, row_count, heads_per_group, head_width
    )
    new_kv = projected[:, :, heads_per_group * head_width :]
    prefill = lax.axis_index("group") == 0
    decode_on = jnp.logical_not(prefill)
    query_pos = lax.axis_index("seq") * row_count + jnp.arange(row_count, dtype=jnp.int32)
    admitted = jnp.repeat(receive, draft_count) > 0
    query_req = queries.reshape(group_count, requests, draft_count, heads_per_group, head_width)
    own_keys = new_kv[..., :head_width].reshape(group_count, requests, draft_count, head_width)
    own_values = new_kv[..., head_width:].reshape(group_count, requests, draft_count, head_width)
    cache_logits = (
        jnp.einsum(
            "gbtph,bugh->gbtpu",
            query_req,
            cache[..., :head_width],
            preferred_element_type=jnp.float32,
        )
        * score_scale
    )
    own_logits = (
        jnp.einsum("gbtph,gbuh->gbtpu", query_req, own_keys, preferred_element_type=jnp.float32)
        * score_scale
    )
    live_cache = (
        (jnp.arange(slot_count, dtype=jnp.int32)[None, :] < cache_len[:, None]) & decode_on
    )[None, :, None, None, :]
    causal = jnp.arange(draft_count)[None, :] <= jnp.arange(draft_count)[:, None]
    live_own = (causal & decode_on)[None, None, :, None, :]
    running_max = jnp.maximum(
        jnp.max(jnp.where(live_cache, cache_logits, MASKED_SCORE), axis=-1),
        jnp.max(jnp.where(live_own, own_logits, MASKED_SCORE), axis=-1),
    )
    cache_weights = jnp.where(live_cache, jnp.exp(cache_logits - running_max[..., None]), 0.0)
    own_weights = jnp.where(live_own, jnp.exp(own_logits - running_max[..., None]), 0.0)
    running_sum = jnp.sum(cache_weights, axis=-1) + jnp.sum(own_weights, axis=-1)
    weighted = jnp.einsum(
        "gbtpu,bugh->gbtph",
        cache_weights.astype(jnp.bfloat16),
        cache[..., head_width:],
        preferred_element_type=jnp.float32,
    )
    weighted = weighted + jnp.einsum(
        "gbtpu,gbuh->gbtph",
        own_weights.astype(jnp.bfloat16),
        own_values,
        preferred_element_type=jnp.float32,
    )
    carried_state = (
        running_max.reshape(group_count, row_count, heads_per_group),
        running_sum.reshape(group_count, row_count, heads_per_group),
        weighted.reshape(group_count, row_count, heads_per_group, head_width),
    )
    assembled = lax.all_gather(new_kv, "seq", axis=1, tiled=True)
    arrived = passed_along(assembled, "group", 1)
    prompt_kv = jnp.where(prefill, assembled, arrived)
    old_max, old_sum, old_weighted = carried_state
    key_count = prompt_kv.shape[1]
    logits = (
        jnp.einsum(
            "grph,gjh->grpj",
            queries,
            prompt_kv[..., :head_width],
            preferred_element_type=jnp.float32,
        )
        * score_scale
    )
    key_pos = jnp.arange(key_count, dtype=jnp.int32)
    allowed = jnp.where(prefill, key_pos[None, :] <= query_pos[:, None], admitted[:, None])[
        None, :, None, :
    ]
    new_max = jnp.maximum(old_max, jnp.max(jnp.where(allowed, logits, MASKED_SCORE), axis=-1))
    weights = jnp.where(allowed, jnp.exp(logits - new_max[..., None]), 0.0)
    rescale = jnp.exp(old_max - new_max)
    new_sum = old_sum * rescale + jnp.sum(weights, axis=-1)
    new_weighted = old_weighted * rescale[..., None] + jnp.einsum(
        "grpj,gjh->grph",
        weights.astype(jnp.bfloat16),
        prompt_kv[..., head_width:],
        preferred_element_type=jnp.float32,
    )
    carried_state = (new_max, new_sum, new_weighted)
    final_max, final_sum, final_weighted = carried_state
    output = (final_weighted / final_sum[..., None]).astype(jnp.bfloat16)
    return jnp.transpose(output, (1, 0, 2, 3)).reshape(
        1, row_count, group_count * heads_per_group * head_width
    )


def solution(mesh):
    def shards(hidden, w_qkv, cache, cache_len, receive):
        head_width = cache.shape[3] // 2
        fits = (
            mesh.shape["group"] == 2
            and mesh.shape["mp"] == 2
            and mesh.shape["seq"] % 2 == 0
            and w_qkv.shape[0] == 4
            and w_qkv.shape[2] == 6 * head_width
            and head_width == 128
            and hidden.shape[1] % (CHUNKS * BLOCK_ROWS) == 0
        )
        run = fast_shards if fits else plain_shards
        return run(hidden, w_qkv, cache, cache_len, receive)

    return jax.shard_map(
        shards,
        mesh=mesh,
        in_specs=(
            P("group", "seq", "mp"),
            P("mp", None, None),
            P("seq", None, "mp", None),
            P("seq"),
            P("seq"),
        ),
        out_specs=P("group", "seq", "mp"),
        check_vma=False,
    )
```

```python
import functools

import jax
import jax.numpy as jnp
from jax import lax
from jax.experimental import pallas as pl
from jax.experimental.pallas import tpu as pltpu
from jax.sharding import PartitionSpec as P

MASKED_SCORE = -1e30
SUB_REQ = 8
LANES = 128
CHUNKS = 2
PAD = 16
SAFE_LOGIT = 60.0
LOG2E = 1.4426950408889634
MIB = 1 << 20
NT = (((1,), (1,)), ((), ()))
NN = (((1,), (0,)), ((), ()))
ANY = pl.BlockSpec(memory_space=pltpu.HBM)
SMALL, LARGE = 1000, 200_000_000_000


def passed_along(block, axis, distance):
    devices = range(lax.axis_size(axis))
    route = [(i - distance, i) for i in devices if i - distance in devices]
    return lax.ppermute(block, axis, route)


def dot(a, b, dims):
    return lax.dot_general(a, b, dims, preferred_element_type=jnp.float32)


def call(kernel, name, grid, prefetch, in_specs, out_specs, out_shape, scratch=(), cost=SMALL, mib=48, aliases=None):
    return pl.pallas_call(
        kernel,
        grid_spec=pltpu.PrefetchScalarGridSpec(
            num_scalar_prefetch=prefetch,
            grid=grid,
            in_specs=in_specs,
            out_specs=out_specs,
            scratch_shapes=list(scratch),
        ),
        out_shape=out_shape,
        input_output_aliases=aliases or {},
        compiler_params=pltpu.CompilerParams(
            dimension_semantics=("arbitrary",) * len(grid), vmem_limit_bytes=mib * MIB
        ),
        cost_estimate=pl.CostEstimate(flops=cost, bytes_accessed=SMALL, transcendentals=0),
        name=name,
    )


def after_all(block, *before):
    return pl.pallas_call(
        lambda *refs: None,
        in_specs=[ANY] * (1 + len(before)),
        out_specs=ANY,
        out_shape=jax.ShapeDtypeStruct(block.shape, block.dtype),
        input_output_aliases={0: 0},
        name="after_all",
    )(block, *before)


def choose_kernel(ids, near, far, *refs):
    refs[-1][...] = jnp.where(ids[2] == 0, near[...], far[...])


def choose(ids, near, far, after):
    whole = pl.BlockSpec(near.shape, lambda i, ids: (0, 0))
    return call(
        choose_kernel,
        "choose",
        (1,),
        1,
        [whole, whole] + [ANY] * len(after),
        whole,
        jax.ShapeDtypeStruct(near.shape, near.dtype),
    )(ids, near, far, *after)


def project_kernel(heads, ids, own, own_s, oth, oth_s, w, *refs):
    q_out, theirs, kv0, kv1, total = refs[-5:]
    gi, half = pl.program_id(0), pl.program_id(1)
    rows = own.shape[0]

    def product(mine, others):
        return dot(jnp.concatenate([mine[...], others[...]], axis=0), w[0], NN)

    @pl.when(half == 0)
    def _():
        total[...] = product(own, own_s)

    @pl.when(half == 1)
    def _():
        res = (total[...] + product(oth, oth_s)).astype(jnp.bfloat16)
        width = res.shape[1] // (heads + 2)
        for side in range(2):
            for h in range(heads):
                q_out[0, side, h * rows : (h + 1) * rows, :] = res[
                    side * rows : (side + 1) * rows, h * width : (h + 1) * width
                ]
        theirs[0] = res[rows:]

        @pl.when(gi == 0)
        def _():
            kv0[...] = res[:, heads * width :]

        @pl.when(gi == 1)
        def _():
            kv1[...] = res[:, heads * width :]


def project(ids, own, own_s, oth, oth_s, w, before, chunk, after, cost):
    rows, width = oth.shape
    columns = w.shape[2]
    kv_cols = columns // 3
    heads = 4
    head_width = kv_cols // 2

    x_specs = [pl.BlockSpec((rows, width), lambda i, half, ids: (chunk, 0))] * 2
    x_specs += [pl.BlockSpec((rows, width), lambda i, half, ids: (0, 0))] * 2
    in_specs = x_specs + [
        pl.BlockSpec((1, width, columns), lambda i, half, ids: (2 * ids[0] + i, half ^ ids[3], 0))
    ]
    args = [ids, own, own_s, oth, oth_s, w]
    aliases = {}
    if before is not None:
        aliases = {len(args): 0}
        in_specs.append(ANY)
        args.append(before)
    whole = pl.BlockSpec((2 * rows, kv_cols), lambda i, half, ids: (0, 0))
    return call(
        functools.partial(project_kernel, heads),
        "project",
        (2, 2),
        1,
        in_specs + [ANY] * len(after),
        [
            pl.BlockSpec((1, 2, heads * rows, head_width), lambda i, half, ids: (i, chunk, 0, 0)),
            pl.BlockSpec((1, rows, columns), lambda i, half, ids: (i, 0, 0)),
            whole,
            whole,
        ],
        [
            jax.ShapeDtypeStruct((2, 2 * CHUNKS, heads * rows, head_width), jnp.bfloat16),
            jax.ShapeDtypeStruct((2, rows, columns), jnp.bfloat16),
            jax.ShapeDtypeStruct((2 * rows, kv_cols), jnp.bfloat16),
            jax.ShapeDtypeStruct((2 * rows, kv_cols), jnp.bfloat16),
        ],
        [pltpu.VMEM((2 * rows, columns), jnp.float32)],
        cost=cost,
        mib=56,
        aliases=aliases,
    )(*args, *after)


def cache_kernel(side, heads, draft, start_req, scale, ids, lens, receive, cache, *refs):
    out = refs[-1]
    _, step_req, slots, both = cache.shape
    width = both // 2
    rows = SUB_REQ * draft
    stacked = heads * rows
    step = pl.program_id(0)
    factor = scale * LOG2E

    @pl.when(ids[2] == 1)
    def _():
        row = lax.broadcasted_iota(jnp.int32, (stacked, slots), 0)
        req_of_row = row % rows // draft
        slot = lax.broadcasted_iota(jnp.int32, (stacked, slots), 1)
        own_row = lax.broadcasted_iota(jnp.int32, (stacked, rows), 0) % rows
        own_key = lax.broadcasted_iota(jnp.int32, (stacked, rows), 1)
        own_bias = jnp.where(
            (own_row // draft == own_key // draft) & (own_key <= own_row), 0.0, MASKED_SCORE
        )
        lane = lax.broadcasted_iota(jnp.int32, (rows, LANES), 1)
        req_of_lane_row = lax.broadcasted_iota(jnp.int32, (rows, LANES), 0) // draft
        chains, biases, flags = [], [], []
        for sub in range(step_req // SUB_REQ):
            req0 = start_req + step * step_req + sub * SUB_REQ
            biases.append(
                jnp.concatenate(
                    [
                        jnp.where((req_of_row == r) & (slot < lens[req0 + r]), 0.0, MASKED_SCORE)
                        for r in range(SUB_REQ)
                    ],
                    axis=1,
                )
            )
            flag = jnp.zeros((rows, LANES), jnp.float32)
            for r in range(SUB_REQ):
                flag = jnp.where(
                    (req_of_lane_row == r) & (receive[req0 + r] > 0) & (lane == heads), 1.0, flag
                )
            flags.append(flag)
            here = slice(sub * rows, (sub + 1) * rows)
            for gi in range(2):
                if side == 0:
                    q, kv_of = refs[0], refs[1 + gi]
                    per_head = q.shape[2] // heads
                    row0 = pl.multiple_of(step * (step_req * draft) + sub * rows, rows)
                    queries = [q[gi, 0, pl.ds(h * per_head + row0, rows), :] for h in range(heads)]
                    own = kv_of[here, :]
                else:
                    block = refs[0][gi, here, :]
                    queries = [block[:, h * width : (h + 1) * width] for h in range(heads)]
                    own = block[:, heads * width :]
                kv = cache[gi, sub * SUB_REQ : (sub + 1) * SUB_REQ].reshape(SUB_REQ * slots, both)
                chains.append((gi, sub, here, jnp.concatenate(queries, axis=0), own, kv))
        s = [dot(q, kv[:, :width], NT) for _, _, _, q, own, kv in chains]
        s_own = [dot(q, own[:, :width], NT) for _, _, _, q, own, kv in chains]
        s = [x * factor + biases[chain[1]] for x, chain in zip(s, chains)]
        s_own = [x * factor + own_bias for x in s_own]
        top = [
            jnp.maximum(jnp.max(a, axis=1, keepdims=True), jnp.max(b, axis=1, keepdims=True))
            for a, b in zip(s, s_own)
        ]
        p = [jnp.exp2(x - t) for x, t in zip(s, top)]
        p_own = [jnp.exp2(x - t) for x, t in zip(s_own, top)]
        total = [
            jnp.sum(a, axis=1, keepdims=True) + jnp.sum(b, axis=1, keepdims=True)
            for a, b in zip(p, p_own)
        ]
        o = [
            dot(a.astype(jnp.bfloat16), kv[:, width:], NN)
            + dot(b.astype(jnp.bfloat16), own[:, width:], NN)
            for a, b, (_, _, _, _, own, kv) in zip(p, p_own, chains)
        ]
        for i, (gi, sub, here, _, _, _) in enumerate(chains):
            scaled = o[i] / total[i]
            lse = top[i] + jnp.log2(total[i])
            extra = flags[sub]
            for h in range(heads):
                part = slice(h * rows, (h + 1) * rows)
                out[gi, here, h * width : (h + 1) * width] = scaled[part]
                extra = jnp.where(lane == h, lse[part], extra)
            out[gi, here, heads * width :] = extra


def cache_attention(side, ids, lens, receive, cache_t, operands, chunk, rows, draft, scale, heads, after, cost):
    _, _, slots, both = cache_t.shape
    width = both // 2
    step_req = 2 * SUB_REQ
    step_rows = step_req * draft
    steps = rows // step_rows
    first = chunk * steps
    if side == 0:
        specs = [
            pl.BlockSpec(
                (2, 1, heads * rows, width), lambda i, ids, lens, receive: (0, 2 * chunk, 0, 0)
            )
        ]
        specs += [pl.BlockSpec((step_rows, both), lambda i, ids, lens, receive: (i, 0))] * 2
    else:
        columns = operands[0].shape[2]
        specs = [
            pl.BlockSpec((2, step_rows, columns), lambda i, ids, lens, receive: (0, i, 0))
        ]

    def cache_map(i, ids, lens, receive):
        return (ids[0] ^ side, (first + i) * ids[2], 0, 0)

    return call(
        functools.partial(cache_kernel, side, heads, draft, chunk * rows // draft, scale),
        "cache_attention",
        (steps,),
        3,
        [pl.BlockSpec((2, step_req, slots, both), cache_map)] + specs + [ANY] * len(after),
        pl.BlockSpec((2, step_rows, heads * width + LANES), lambda i, ids, lens, receive: (0, i, 0)),
        jax.ShapeDtypeStruct((2, rows, heads * width + LANES), jnp.float32),
        cost=cost,
    )(ids, lens, receive, cache_t, *operands, *after)


def prompt_kernel(gi, heads, first, last, slots_n, key_start, rows_core, scale, ids, stats, *refs):
    refs = list(refs)
    q, own = refs.pop(0), refs.pop(0)
    arrived = [refs.pop(0) for _ in range(slots_n)]
    if not first:
        acc_in, m_in = refs.pop(0), refs.pop(0)
    if last:
        parts = [refs.pop(0) for _ in range(2 * CHUNKS)]
        outs = refs[-10:-8]
    else:
        acc_out, m_out, stats_out = refs[-11:-8]
    kvbuf, kd, vt, acc, m_ref, part_ref, fast, sems = refs[-8:]
    blk = pl.program_id(0)
    core, z, grp = ids[0], ids[1], ids[2]
    chips = slots_n // 2
    place = jnp.where(grp == 0, z, slots_n - 1 - z)
    keys = kvbuf.shape[1]
    size = keys // 2
    stacked, width = q.shape[2:]
    rows = stacked // heads

    @pl.when(blk == 0)
    def _():
        def each(act):
            for t in range(slots_n):
                r = lax.rem(place - t + slots_n, slots_n)
                chip = jnp.where(r < chips, r, slots_n - 1 - r)

                @pl.when((r < chips) == (gi == 0))
                def _():
                    act(pltpu.make_async_copy(arrived[t], kvbuf.at[chip], sems.at[t]))

        each(lambda copy: copy.start())
        row = lax.broadcasted_iota(jnp.int32, (PAD, keys), 0)
        ones = jnp.where(row == 0, 1.0, 0.0).astype(jnp.bfloat16)
        all_ones = jnp.ones((width, LANES), jnp.bfloat16)

        def place_block(c, kv, longest):
            k = kv[:, :width]
            here = slice(c * keys, (c + 1) * keys)
            kd[here, :width] = k
            kd[here, width:] = k
            vt[:width, here] = kv[:, width:].T
            vt[width:, here] = ones
            wide = k.astype(jnp.float32)
            norms = dot((wide * wide).astype(jnp.bfloat16), all_ones, NN)
            return jnp.maximum(longest, jnp.max(norms, axis=0, keepdims=True))

        longest = place_block(chips, own[...], jnp.full((1, LANES), stats[1], jnp.float32))
        each(lambda copy: copy.wait())
        for c in range(chips):
            longest = place_block(c, kvbuf[c], longest)
        top = jnp.max(longest)
        fast[0] = jnp.where(
            top * stats[0] * (1.02 * scale * scale) <= SAFE_LOGIT * SAFE_LOGIT, 1.0, 0.0
        )
        if not last:
            stats_out[0] = stats[0]
            stats_out[1] = top

    if first:
        acc[...] = jnp.zeros_like(acc)
        m_ref[...] = jnp.where(fast[0] > 0, 0.0, jnp.full_like(m_ref, MASKED_SCORE))
    else:
        acc[...] = acc_in[0]
        m_ref[...] = m_in[0]

    wide = q[0, 0].astype(jnp.float32) * (scale * LOG2E)
    high = wide.astype(jnp.bfloat16)
    low = (wide - high.astype(jnp.float32)).astype(jnp.bfloat16)
    q2 = jnp.concatenate([high, low], axis=1)

    side = blk % 2
    pos = (core ^ side) * rows_core + blk // 2 * rows
    full_n = jnp.where(grp == 0, z, chips)
    own_on = (grp == 0) & (key_start <= pos + rows - 1)

    def admitted():
        shape = (keys, stacked)
        key = lax.broadcasted_iota(jnp.int32, shape, 0)
        key_core = jnp.where(key >= size, 1 - core, core)
        key_pos = key_start + key_core * rows_core + jnp.where(key >= size, key - size, key)
        row_pos = pos + lax.broadcasted_iota(jnp.int32, shape, 1) % rows
        return key_pos <= row_pos

    def scores(at, n):
        return dot(kd[pl.ds(at, n * keys)], q2, NT)

    def weighted(at, n, p):
        return dot(vt[:, pl.ds(at, n * keys)], p.astype(jnp.bfloat16), NN)

    @pl.when(fast[0] > 0)
    def _():
        for n in range(1, chips + 1):

            @pl.when(full_n == n)
            def _(n=n):
                acc[...] = acc[...] + weighted(0, n, jnp.exp2(scores(0, n)))

        @pl.when(own_on)
        def _():
            p = jnp.where(admitted(), jnp.exp2(scores(chips * keys, 1)), 0.0)
            acc[...] = acc[...] + weighted(chips * keys, 1, p)

    @pl.when(fast[0] == 0)
    def _():
        def visit(at, s):
            old = m_ref[:1]
            new = jnp.maximum(old, jnp.max(s, axis=0, keepdims=True))
            acc[...] = acc[...] * jnp.exp2(old - new) + weighted(at, 1, jnp.exp2(s - new))
            m_ref[...] = jnp.broadcast_to(new, m_ref.shape)

        def body(c, carry):
            at = pl.multiple_of(c * keys, keys)
            visit(at, scores(at, 1))
            return carry

        lax.fori_loop(0, full_n, body, 0)

        @pl.when(own_on)
        def _():
            s = scores(chips * keys, 1)
            visit(chips * keys, jnp.where(admitted(), s, MASKED_SCORE))

    if not last:
        acc_out[0] = acc[...]
        m_out[0] = m_ref[...]
        return
    total = acc[width : width + 1]

    def write(h, value):
        columns = slice(h * width, (h + 1) * width)
        value = value.astype(jnp.bfloat16)

        @pl.when(side == 0)
        def _():
            outs[0][:, columns] = value

        @pl.when(side == 1)
        def _():
            outs[1][:, columns] = value

    @pl.when(grp == 0)
    def _():
        o_all = (acc[:width] * (1.0 / total)).T
        for h in range(heads):
            write(h, o_all[h * rows : (h + 1) * rows])

    @pl.when(grp == 1)
    def _():
        for i in range(2 * CHUNKS):

            @pl.when(blk == i)
            def _(i=i):
                part_ref[...] = parts[i][0]

        extra = part_ref[:, heads * width :].T
        lse_c = jnp.concatenate([extra[h : h + 1] for h in range(heads)], axis=1)
        flag = jnp.concatenate([extra[heads : heads + 1]] * heads, axis=1)
        o_c = jnp.concatenate(
            [part_ref[:, h * width : (h + 1) * width].T for h in range(heads)], axis=1
        )
        lse_p = jnp.where(flag > 0, m_ref[:1] + jnp.log2(total), MASKED_SCORE)
        top = jnp.maximum(lse_p, lse_c)
        w_p = jnp.exp2(lse_p - top)
        w_c = jnp.exp2(lse_c - top)
        rest = 1.0 / (w_p + w_c)
        merged = (acc[:width] * (w_p * rest / total) + o_c * (w_c * rest)).T
        for h in range(heads):
            write(h, merged[h * rows : (h + 1) * rows])


def prompt_attention(gi, heads, ids, stats, q, own, arrived, state, parts, chunk, rows_core, scale, after, cost):
    slots_n = len(arrived)
    _, blocks, stacked, width = q.shape
    first, last = state is None, parts is not None
    rows = stacked // heads
    keys = 2 * rows
    chips = slots_n // 2

    acc_shape = (blocks, width + PAD, stacked)
    m_shape = (blocks, 8, stacked)
    acc_spec = pl.BlockSpec((1,) + acc_shape[1:], lambda blk, ids: (blk, 0, 0))
    m_spec = pl.BlockSpec((1,) + m_shape[1:], lambda blk, ids: (blk, 0, 0))
    stat_spec = pl.BlockSpec(memory_space=pltpu.SMEM)
    in_specs = [
        stat_spec,
        pl.BlockSpec((1, 1, stacked, width), lambda blk, ids: (gi, blk, 0, 0)),
        pl.BlockSpec((keys, 2 * width), lambda blk, ids: (0, 0)),
    ]
    in_specs += [ANY] * slots_n
    args = [ids, stats, q, own, *arrived]
    if not first:
        in_specs += [acc_spec, m_spec]
        args += list(state)
    part_shape = (rows, heads * width + LANES)
    if last:
        in_specs += [pl.BlockSpec((1,) + part_shape, lambda blk, ids: (gi, 0, 0))] * len(parts)
        args += list(parts)
        out_specs = [pl.BlockSpec((rows, heads * width), lambda blk, ids: (blk // 2, 0))] * 2
        out_shape = [jax.ShapeDtypeStruct((rows_core, heads * width), jnp.bfloat16)] * 2
    else:
        out_specs = [acc_spec, m_spec, stat_spec]
        out_shape = [
            jax.ShapeDtypeStruct(acc_shape, jnp.float32),
            jax.ShapeDtypeStruct(m_shape, jnp.float32),
            jax.ShapeDtypeStruct((2,), jnp.float32),
        ]
    in_specs += [ANY] * len(after)
    return call(
        functools.partial(
            prompt_kernel, gi, heads, first, last, slots_n, chunk * rows, rows_core, scale
        ),
        "prompt_attention",
        (blocks,),
        1,
        in_specs,
        out_specs,
        out_shape,
        [
            pltpu.VMEM((chips, keys, 2 * width), jnp.bfloat16),
            pltpu.VMEM(((chips + 1) * keys, 2 * width), jnp.bfloat16),
            pltpu.VMEM((width + PAD, (chips + 1) * keys), jnp.bfloat16),
            pltpu.VMEM((width + PAD, stacked), jnp.float32),
            pltpu.VMEM((8, stacked), jnp.float32),
            pltpu.VMEM(part_shape, jnp.float32),
            pltpu.SMEM((1,), jnp.float32),
            pltpu.SemaphoreType.DMA((slots_n,)),
        ],
        cost=cost,
        mib=56,
    )(*args, *after)


def fast_shards(hidden, w_qkv, cache, cache_len, receive):
    head_width = cache.shape[3] // 2
    heads = w_qkv.shape[2] // head_width - 2
    rows_core = hidden.shape[1]
    rows = rows_core // CHUNKS
    draft = rows_core // cache.shape[0]
    scale = head_width ** (-0.5)
    seq_n = lax.axis_size("seq")
    chips = seq_n // 2
    ring_n = 2 * chips

    seq_i, group_i, mp_i = lax.axis_index("seq"), lax.axis_index("group"), lax.axis_index("mp")
    core = seq_i % 2
    ids = jnp.stack([core, seq_i // 2, group_i, mp_i]).astype(jnp.int32)

    mp_swap = [(0, 1), (1, 0)]
    core_swap = [(i, i ^ 1) for i in range(seq_n)]
    ring = [(0, k) for k in range(chips)] + [(1, chips - 1 - k) for k in range(chips)]
    index = [[g * seq_n + 2 * k + c for c in range(2)] for g, k in ring]
    up = [(index[r][c], index[(r + 1) % ring_n][c]) for r in range(ring_n) for c in range(2)]
    down = [(index[r][c], index[r - 1][c]) for r in range(ring_n) for c in range(2)]

    def swap_cores(x):
        return lax.ppermute(x, "seq", core_swap)

    def round_the_ring(block):
        ups, downs = [block], [block]
        for step in range(ring_n // 2):
            ups.append(lax.ppermute(ups[-1], ("group", "seq"), up))
            if step < ring_n // 2 - 1:
                downs.append(lax.ppermute(downs[-1], ("group", "seq"), down))
        return ups, downs, ups + downs[:0:-1]

    def step_of(rings, step):
        step = min(step, ring_n // 2)
        return [rings[0][step]] + ([rings[1][step]] if step < ring_n // 2 else [])

    own = hidden[0]
    oth = [lax.ppermute(own[c * rows : (c + 1) * rows], "mp", mp_swap) for c in range(CHUNKS)]
    own_s = swap_cores(own)
    cache_t = jnp.transpose(cache, (2, 0, 1, 3))

    def cached(side, chunk, operands, after):
        return cache_attention(
            side, ids, cache_len, receive, cache_t, operands, chunk, rows, draft, scale, heads, after, LARGE
        )

    def projected(chunk, before, cost):
        return project(ids, own, own_s, oth[chunk], swap_cores(oth[chunk]), w_qkv, before, chunk, [], cost)

    oth[0] = after_all(oth[0], cache_t)
    q, theirs_0, kv0_0, kv1_0 = projected(0, None, SMALL)
    crossed_0 = lax.ppermute(kv1_0, "group", [(0, 1)])
    swapped_0 = swap_cores(theirs_0)
    near_0 = cached(0, 0, (q, kv0_0, kv1_0), [])
    ring_0 = round_the_ring(choose(ids, kv0_0, crossed_0, [near_0]))

    oth[1] = after_all(oth[1], near_0)
    q, theirs_1, kv0_1, kv1_1 = projected(1, q, LARGE)
    crossed_1 = lax.ppermute(kv1_1, "group", [(0, 1)])
    swapped_1 = swap_cores(theirs_1)
    far_0 = cached(1, 0, (swapped_0,), [kv0_1] + step_of(ring_0, 1))
    ring_1 = round_the_ring(choose(ids, kv0_1, crossed_1, [far_0]))
    away_0 = swap_cores(far_0)
    near_1 = cached(0, 1, (q, kv0_1, kv1_1), [ring_1[0][0]] + step_of(ring_0, 2))
    far_1 = cached(1, 1, (swapped_1,), [near_1, away_0] + step_of(ring_1, 1) + step_of(ring_0, 3))
    away_1 = swap_cores(far_1)
    parts = [near_0, away_0, near_1, away_1]

    longest = jnp.max(jnp.sum(jnp.square(q.astype(jnp.float32)), axis=-1))
    stats = [jnp.stack([longest, jnp.zeros_like(longest)])] * 2

    def attend(gi, chunk, state, after):
        own_kv = ((kv0_0, kv1_0), (kv0_1, kv1_1))[chunk][gi]
        arrived = (ring_0, ring_1)[chunk][2]
        return prompt_attention(
            gi,
            heads,
            ids,
            stats[gi] if state is None else state[2],
            q,
            own_kv,
            arrived,
            None if state is None else state[:2],
            None if state is None else parts,
            chunk,
            rows_core,
            scale,
            after,
            LARGE,
        )

    state_0 = attend(0, 0, None, [far_1] + step_of(ring_1, 2))
    state_1 = attend(1, 0, None, [state_0[0], away_1] + step_of(ring_1, 3))
    out_0 = attend(0, 1, state_0, [state_1[0]])
    out_1 = attend(1, 1, state_1, [out_0[0]])
    mine = [out_0[0], out_1[0]]
    back = [swap_cores(out_0[1]), swap_cores(out_1[1])]
    return jnp.where(
        core == 0,
        jnp.concatenate(mine + back, axis=1),
        jnp.concatenate(back + mine, axis=1),
    )[None]


def plain_shards(hidden, w_qkv, cache, cache_len, receive):
    group_count = w_qkv.shape[0]
    column_count = w_qkv.shape[2]
    head_width = cache.shape[3] // 2
    heads_per_group = column_count // head_width - 2
    row_count = hidden.shape[1]
    requests = cache.shape[0]
    draft_count = row_count // requests
    slot_count = cache.shape[1]
    score_scale = head_width ** (-0.5)
    projected = jnp.einsum(
        "rd,gdc->grc",
        lax.all_gather(hidden, "mp", axis=2, tiled=True)[0],
        w_qkv,
        preferred_element_type=jnp.float32,
    ).astype(jnp.bfloat16)
    queries = projected[:, :, : heads_per_group * head_width].reshape(
        group_count, row_count, heads_per_group, head_width
    )
    new_kv = projected[:, :, heads_per_group * head_width :]
    prefill = lax.axis_index("group") == 0
    decode_on = jnp.logical_not(prefill)
    query_pos = lax.axis_index("seq") * row_count + jnp.arange(row_count, dtype=jnp.int32)
    admitted = jnp.repeat(receive, draft_count) > 0
    query_req = queries.reshape(group_count, requests, draft_count, heads_per_group, head_width)
    own_keys = new_kv[..., :head_width].reshape(group_count, requests, draft_count, head_width)
    own_values = new_kv[..., head_width:].reshape(group_count, requests, draft_count, head_width)
    cache_logits = (
        jnp.einsum(
            "gbtph,bugh->gbtpu",
            query_req,
            cache[..., :head_width],
            preferred_element_type=jnp.float32,
        )
        * score_scale
    )
    own_logits = (
        jnp.einsum("gbtph,gbuh->gbtpu", query_req, own_keys, preferred_element_type=jnp.float32)
        * score_scale
    )
    live_cache = (
        (jnp.arange(slot_count, dtype=jnp.int32)[None, :] < cache_len[:, None]) & decode_on
    )[None, :, None, None, :]
    causal = jnp.arange(draft_count)[None, :] <= jnp.arange(draft_count)[:, None]
    live_own = (causal & decode_on)[None, None, :, None, :]
    running_max = jnp.maximum(
        jnp.max(jnp.where(live_cache, cache_logits, MASKED_SCORE), axis=-1),
        jnp.max(jnp.where(live_own, own_logits, MASKED_SCORE), axis=-1),
    )
    cache_weights = jnp.where(live_cache, jnp.exp(cache_logits - running_max[..., None]), 0.0)
    own_weights = jnp.where(live_own, jnp.exp(own_logits - running_max[..., None]), 0.0)
    running_sum = jnp.sum(cache_weights, axis=-1) + jnp.sum(own_weights, axis=-1)
    weighted = jnp.einsum(
        "gbtpu,bugh->gbtph",
        cache_weights.astype(jnp.bfloat16),
        cache[..., head_width:],
        preferred_element_type=jnp.float32,
    )
    weighted = weighted + jnp.einsum(
        "gbtpu,gbuh->gbtph",
        own_weights.astype(jnp.bfloat16),
        own_values,
        preferred_element_type=jnp.float32,
    )
    carried_state = (
        running_max.reshape(group_count, row_count, heads_per_group),
        running_sum.reshape(group_count, row_count, heads_per_group),
        weighted.reshape(group_count, row_count, heads_per_group, head_width),
    )
    assembled = lax.all_gather(new_kv, "seq", axis=1, tiled=True)
    arrived = passed_along(assembled, "group", 1)
    prompt_kv = jnp.where(prefill, assembled, arrived)
    old_max, old_sum, old_weighted = carried_state
    key_count = prompt_kv.shape[1]
    logits = (
        jnp.einsum(
            "grph,gjh->grpj",
            queries,
            prompt_kv[..., :head_width],
            preferred_element_type=jnp.float32,
        )
        * score_scale
    )
    key_pos = jnp.arange(key_count, dtype=jnp.int32)
    allowed = jnp.where(prefill, key_pos[None, :] <= query_pos[:, None], admitted[:, None])[
        None, :, None, :
    ]
    new_max = jnp.maximum(old_max, jnp.max(jnp.where(allowed, logits, MASKED_SCORE), axis=-1))
    weights = jnp.where(allowed, jnp.exp(logits - new_max[..., None]), 0.0)
    rescale = jnp.exp(old_max - new_max)
    new_sum = old_sum * rescale + jnp.sum(weights, axis=-1)
    new_weighted = old_weighted * rescale[..., None] + jnp.einsum(
        "grpj,gjh->grph",
        weights.astype(jnp.bfloat16),
        prompt_kv[..., head_width:],
        preferred_element_type=jnp.float32,
    )
    carried_state = (new_max, new_sum, new_weighted)
    final_max, final_sum, final_weighted = carried_state
    output = (final_weighted / final_sum[..., None]).astype(jnp.bfloat16)
    return jnp.transpose(output, (1, 0, 2, 3)).reshape(
        1, row_count, group_count * heads_per_group * head_width
    )


def solution(mesh):
    def shards(hidden, w_qkv, cache, cache_len, receive):
        head_width = cache.shape[3] // 2
        fits = (
            mesh.shape["group"] == 2
            and mesh.shape["mp"] == 2
            and mesh.shape["seq"] % 2 == 0
            and w_qkv.shape[0] == 4
            and w_qkv.shape[2] == 6 * head_width
            and head_width == 128
            and hidden.shape[1] % (CHUNKS * 2 * SUB_REQ * 4) == 0
            and hidden.shape[1] == 4 * cache.shape[0]
        )
        run = fast_shards if fits else plain_shards
        return run(hidden, w_qkv, cache, cache_len, receive)

    return jax.shard_map(
        shards,
        mesh=mesh,
        in_specs=(
            P("group", "seq", "mp"),
            P("mp", None, None),
            P("seq", None, "mp", None),
            P("seq"),
            P("seq"),
        ),
        out_specs=P("group", "seq", "mp"),
        check_vma=False,
    )
```

```python
import functools

import jax
import jax.numpy as jnp
from jax import lax
from jax.experimental import pallas as pl
from jax.experimental.pallas import tpu as pltpu
from jax.sharding import PartitionSpec as P

MASKED_SCORE = -1e30
SUB_REQ = 8
LANES = 128
CHUNKS = 2
PAD = 16
SAFE_LOGIT = 60.0
LOG2E = 1.4426950408889634
MIB = 1 << 20
NT = (((1,), (1,)), ((), ()))
NN = (((1,), (0,)), ((), ()))
ANY = pl.BlockSpec(memory_space=pltpu.HBM)
SMALL, LARGE = 1000, 200_000_000_000


def passed_along(block, axis, distance):
    devices = range(lax.axis_size(axis))
    route = [(i - distance, i) for i in devices if i - distance in devices]
    return lax.ppermute(block, axis, route)


def dot(a, b, dims):
    return lax.dot_general(a, b, dims, preferred_element_type=jnp.float32)


def call(kernel, name, grid, prefetch, in_specs, out_specs, out_shape, scratch=(), cost=SMALL, mib=48, aliases=None):
    made = pl.pallas_call(
        kernel,
        grid_spec=pltpu.PrefetchScalarGridSpec(
            num_scalar_prefetch=prefetch,
            grid=grid,
            in_specs=in_specs,
            out_specs=out_specs,
            scratch_shapes=list(scratch),
        ),
        out_shape=out_shape,
        input_output_aliases=aliases or {},
        compiler_params=pltpu.CompilerParams(
            dimension_semantics=("arbitrary",) * len(grid), vmem_limit_bytes=mib * MIB
        ),
        cost_estimate=pl.CostEstimate(flops=cost, bytes_accessed=SMALL, transcendentals=0),
        name=name,
    )

    def on(*args):
        kept = [pltpu.with_memory_space_constraint(x, pltpu.HBM) for x in args[prefetch:]]
        return made(*args[:prefetch], *kept)

    return on


def after_all(block, *before):
    return pl.pallas_call(
        lambda *refs: None,
        in_specs=[ANY] * (1 + len(before)),
        out_specs=ANY,
        out_shape=jax.ShapeDtypeStruct(block.shape, block.dtype),
        input_output_aliases={0: 0},
        name="after_all",
    )(block, *before)


def longest_row(x):
    wide = x.astype(jnp.float32)
    return jnp.max(jnp.sum(wide * wide, axis=1, keepdims=True), axis=0, keepdims=True)


def project_kernel(heads, ids, own, own_s, oth, oth_s, w, *refs):
    q_out, theirs, mine_kv, norms, kv0, kv1, total, top_rows = refs[-8:]
    gi, half = pl.program_id(0), pl.program_id(1)
    rows = own.shape[0]

    def product(mine, others):
        return dot(jnp.concatenate([mine[...], others[...]], axis=0), w[0], NN)

    @pl.when(half == 0)
    def _():
        total[...] = product(own, own_s)

    @pl.when(half == 1)
    def _():
        width = w.shape[2] // (heads + 2)
        longest = jnp.zeros((1, 1), jnp.float32)
        both = (total[...] + product(oth, oth_s)).astype(jnp.bfloat16)
        for side in range(2):
            here = slice(side * rows, (side + 1) * rows)
            res = both[here]
            for h in range(heads):
                q = res[:, h * width : (h + 1) * width]
                q_out[0, side, h * rows : (h + 1) * rows, :] = q
                longest = jnp.maximum(longest, longest_row(q))
            if side == 0:
                mine_kv[0] = res[:, heads * width :]
            else:
                theirs[0] = res

            def ring_form(out):
                k = res[:, heads * width : (heads + 1) * width]
                out[here, :width] = k
                for tile in range(rows // width):
                    lo = tile * width
                    out[side * rows + lo : side * rows + lo + width, width:] = res[
                        lo : lo + width, (heads + 1) * width :
                    ].T
                top = jnp.broadcast_to(longest_row(k) * 1.01, (PAD // 2, 2 * width))
                low = 2 * rows + side * (PAD // 2)
                top_rows[low - 2 * rows : low - 2 * rows + PAD // 2] = top

            @pl.when(gi == 0)
            def _():
                ring_form(kv0)

            @pl.when(gi == 1)
            def _():
                ring_form(kv1)

        norms[0] = jnp.broadcast_to(longest, norms.shape[1:])
        bound = top_rows[...].astype(jnp.bfloat16)

        @pl.when(gi == 0)
        def _():
            kv0[2 * rows :] = bound

        @pl.when(gi == 1)
        def _():
            kv1[2 * rows :] = bound


def project(ids, own, own_s, oth, oth_s, w, before, chunk, after, cost):
    rows, width = oth.shape
    columns = w.shape[2]
    kv_cols = columns // 3
    heads = 4
    head_width = kv_cols // 2

    x_specs = [pl.BlockSpec((rows, width), lambda i, half, ids: (chunk, 0))] * 2
    x_specs += [pl.BlockSpec((rows, width), lambda i, half, ids: (0, 0))] * 2
    in_specs = x_specs + [
        pl.BlockSpec((1, width, columns), lambda i, half, ids: (2 * ids[0] + i, half ^ ids[3], 0))
    ]
    args = [ids, own, own_s, oth, oth_s, w]
    aliases = {}
    if before is not None:
        aliases = {len(args): 0}
        in_specs.append(ANY)
        args.append(before)
    ring_shape = (2 * rows + PAD, kv_cols)
    whole = pl.BlockSpec(ring_shape, lambda i, half, ids: (0, 0))
    return call(
        functools.partial(project_kernel, heads),
        "project",
        (2, 2),
        1,
        in_specs + [ANY] * len(after),
        [
            pl.BlockSpec((1, 2, heads * rows, head_width), lambda i, half, ids: (i, chunk, 0, 0)),
            pl.BlockSpec((1, rows, columns), lambda i, half, ids: (i, 0, 0)),
            pl.BlockSpec((1, rows, kv_cols), lambda i, half, ids: (i, 0, 0)),
            pl.BlockSpec((1, 8, LANES), lambda i, half, ids: (i, 0, 0)),
            whole,
            whole,
        ],
        [
            jax.ShapeDtypeStruct((2, 2 * CHUNKS, heads * rows, head_width), jnp.bfloat16),
            jax.ShapeDtypeStruct((2, rows, columns), jnp.bfloat16),
            jax.ShapeDtypeStruct((2, rows, kv_cols), jnp.bfloat16),
            jax.ShapeDtypeStruct((2, 8, LANES), jnp.float32),
            jax.ShapeDtypeStruct(ring_shape, jnp.bfloat16),
            jax.ShapeDtypeStruct(ring_shape, jnp.bfloat16),
        ],
        [
            pltpu.VMEM((2 * rows, columns), jnp.float32),
            pltpu.VMEM((PAD, kv_cols), jnp.float32),
        ],
        cost=cost,
        mib=56,
        aliases=aliases,
    )(*args, *after)


def cache_kernel(side, heads, draft, start_req, first_step, scale, ids, lens, receive, cache, *refs):
    out = refs[-1]
    _, step_req, slots, both = cache.shape
    width = both // 2
    rows = SUB_REQ * draft
    stacked = heads * rows
    step = pl.program_id(0) + first_step
    factor = scale * LOG2E

    @pl.when(ids[2] == 1)
    def _():
        row = lax.broadcasted_iota(jnp.int32, (stacked, slots), 0)
        req_of_row = row % rows // draft
        slot = lax.broadcasted_iota(jnp.int32, (stacked, slots), 1)
        own_row = lax.broadcasted_iota(jnp.int32, (stacked, rows), 0) % rows
        own_key = lax.broadcasted_iota(jnp.int32, (stacked, rows), 1)
        own_bias = jnp.where(
            (own_row // draft == own_key // draft) & (own_key <= own_row), 0.0, MASKED_SCORE
        )
        lane = lax.broadcasted_iota(jnp.int32, (rows, LANES), 1)
        req_of_lane_row = lax.broadcasted_iota(jnp.int32, (rows, LANES), 0) // draft
        chains, biases, flags = [], [], []
        for sub in range(step_req // SUB_REQ):
            req0 = start_req + step * step_req + sub * SUB_REQ
            biases.append(
                jnp.concatenate(
                    [
                        jnp.where((req_of_row == r) & (slot < lens[req0 + r]), 0.0, MASKED_SCORE)
                        for r in range(SUB_REQ)
                    ],
                    axis=1,
                )
            )
            flag = jnp.zeros((rows, LANES), jnp.float32)
            for r in range(SUB_REQ):
                flag = jnp.where(
                    (req_of_lane_row == r) & (receive[req0 + r] > 0) & (lane == heads), 1.0, flag
                )
            flags.append(flag)
            here = slice(sub * rows, (sub + 1) * rows)
            for gi in range(2):
                if side == 0:
                    q = refs[0]
                    per_head = q.shape[2] // heads
                    row0 = pl.multiple_of(step * (step_req * draft) + sub * rows, rows)
                    queries = [q[gi, 0, pl.ds(h * per_head + row0, rows), :] for h in range(heads)]
                    own = refs[1][gi, here, :]
                else:
                    block = refs[0][gi, here, :]
                    queries = [block[:, h * width : (h + 1) * width] for h in range(heads)]
                    own = block[:, heads * width :]
                kv = cache[gi, sub * SUB_REQ : (sub + 1) * SUB_REQ].reshape(SUB_REQ * slots, both)
                chains.append((gi, sub, here, jnp.concatenate(queries, axis=0), own, kv))
        s = [dot(q, kv[:, :width], NT) for _, _, _, q, own, kv in chains]
        s_own = [dot(q, own[:, :width], NT) for _, _, _, q, own, kv in chains]
        s = [x * factor + biases[chain[1]] for x, chain in zip(s, chains)]
        s_own = [x * factor + own_bias for x in s_own]
        top = [
            jnp.maximum(jnp.max(a, axis=1, keepdims=True), jnp.max(b, axis=1, keepdims=True))
            for a, b in zip(s, s_own)
        ]
        p = [jnp.exp2(x - t) for x, t in zip(s, top)]
        p_own = [jnp.exp2(x - t) for x, t in zip(s_own, top)]
        total = [
            jnp.sum(a, axis=1, keepdims=True) + jnp.sum(b, axis=1, keepdims=True)
            for a, b in zip(p, p_own)
        ]
        o = [
            dot(a.astype(jnp.bfloat16), kv[:, width:], NN)
            + dot(b.astype(jnp.bfloat16), own[:, width:], NN)
            for a, b, (_, _, _, _, own, kv) in zip(p, p_own, chains)
        ]
        for i, (gi, sub, here, _, _, _) in enumerate(chains):
            scaled = o[i] / total[i]
            lse = top[i] + jnp.log2(total[i])
            extra = flags[sub]
            for h in range(heads):
                part = slice(h * rows, (h + 1) * rows)
                out[gi, here, h * width : (h + 1) * width] = scaled[part]
                extra = jnp.where(lane == h, lse[part], extra)
            out[gi, here, heads * width :] = extra


def cache_attention(
    side, ids, lens, receive, cache_t, operands, chunk, rows, draft, scale, heads, after, cost, span=None, before=None
):
    _, _, slots, both = cache_t.shape
    width = both // 2
    step_req = 2 * SUB_REQ
    step_rows = step_req * draft
    steps = rows // step_rows
    lo, hi = span or (0, steps)
    first = chunk * steps + lo
    if side == 0:
        specs = [
            pl.BlockSpec(
                (2, 1, heads * rows, width), lambda i, ids, lens, receive: (0, 2 * chunk, 0, 0)
            )
        ]
        specs += [pl.BlockSpec((2, step_rows, both), lambda i, ids, lens, receive: (0, lo + i, 0))]
    else:
        columns = operands[0].shape[2]
        specs = [
            pl.BlockSpec((2, step_rows, columns), lambda i, ids, lens, receive: (0, lo + i, 0))
        ]

    aliases = {}
    if before is not None:
        aliases = {4 + len(operands) + len(after): 0}
        after = [*after, before]

    def cache_map(i, ids, lens, receive):
        return (ids[0] ^ side, (first + i) * ids[2], 0, 0)

    return call(
        functools.partial(cache_kernel, side, heads, draft, chunk * rows // draft, lo, scale),
        "cache_attention",
        (hi - lo,),
        3,
        [pl.BlockSpec((2, step_req, slots, both), cache_map)] + specs + [ANY] * len(after),
        pl.BlockSpec(
            (2, step_rows, heads * width + LANES), lambda i, ids, lens, receive: (0, lo + i, 0)
        ),
        jax.ShapeDtypeStruct((2, rows, heads * width + LANES), jnp.float32),
        cost=cost,
        aliases=aliases,
    )(ids, lens, receive, cache_t, *operands, *after)


def prompt_kernel(heads, slots_n, rows_core, scale, ids, *refs):
    refs = list(refs)
    norms = [refs.pop(0) for _ in range(CHUNKS)]
    q = refs.pop(0)
    own = [[refs.pop(0), refs.pop(0)] for _ in range(CHUNKS)]
    arrived = [[refs.pop(0) for _ in range(slots_n)] for _ in range(CHUNKS)]
    parts = [refs.pop(0) for _ in range(2 * CHUNKS)]
    outs = refs[-10:-8]
    kvbuf, kd, vt, acc, m_ref, part_ref, fast, sems = refs[-8:]
    gi, blk = pl.program_id(0), pl.program_id(1)
    core, z, grp = ids[0], ids[1], ids[2]
    chips = slots_n // 2
    place = jnp.where(grp == 0, z, slots_n - 1 - z)
    keys = kvbuf.shape[3] - PAD
    stacked, width = q.shape[2:]
    rows = stacked // heads

    def each(act):
        for c in range(CHUNKS):
            for t in range(slots_n):
                r = lax.rem(place - t + slots_n, slots_n)
                chip = jnp.where(r < chips, r, slots_n - 1 - r)
                lane = jnp.where(r < chips, 0, 1)
                act(pltpu.make_async_copy(arrived[c][t], kvbuf.at[lane, c, chip], sems.at[c, t]))

    def place_block(c, at, block):
        k = block[:keys, :width]
        kd[c, at * keys : (at + 1) * keys, :width] = k
        kd[c, at * keys : (at + 1) * keys, width:] = k
        for lo in range(0, keys, width):
            vt[c, :width, at * keys + lo : at * keys + lo + width] = block[lo : lo + width, width:]
        return block[keys:, :].astype(jnp.float32)

    @pl.when((gi == 0) & (blk == 0))
    def _():
        each(lambda copy: copy.start())
        row = lax.broadcasted_iota(jnp.int32, (PAD, vt.shape[2]), 0)
        for c in range(CHUNKS):
            vt[c, width:, :] = jnp.where(row == 0, 1.0, 0.0).astype(jnp.bfloat16)
        each(lambda copy: copy.wait())

    @pl.when(blk == 0)
    def _():
        longest = jnp.zeros((PAD, 2 * width), jnp.float32)
        for c in range(CHUNKS):
            for at in range(chips):
                longest = jnp.maximum(longest, place_block(c, at, kvbuf.at[gi, c, at]))
            for g in range(2):

                @pl.when(gi == g)
                def _(c=c, g=g):
                    part_ref[:PAD, : 2 * width] = place_block(c, chips, own[c][g])

            longest = jnp.maximum(longest, part_ref[:PAD, : 2 * width])
        top_q = norms[0][...]
        for other in norms[1:]:
            top_q = jnp.maximum(top_q, other[...])
        fast[0] = jnp.where(
            jnp.max(longest) * jnp.max(top_q) * (1.02 * scale * scale)
            <= SAFE_LOGIT * SAFE_LOGIT,
            1.0,
            0.0,
        )

    acc[...] = jnp.zeros_like(acc)
    m_ref[...] = jnp.where(fast[0] > 0, 0.0, jnp.full_like(m_ref, MASKED_SCORE))

    wide = q[0, 0].astype(jnp.float32) * (scale * LOG2E)
    high = wide.astype(jnp.bfloat16)
    low = (wide - high.astype(jnp.float32)).astype(jnp.bfloat16)
    q2 = jnp.concatenate([high, low], axis=1)

    side = blk % 2
    pos = (core ^ side) * rows_core + blk // 2 * rows
    full_n = jnp.where(grp == 0, z, chips)

    def admitted(key_start):
        shape = (keys, stacked)
        key = lax.broadcasted_iota(jnp.int32, shape, 0)
        key_core = jnp.where(key >= rows, 1 - core, core)
        key_pos = key_start + key_core * rows_core + jnp.where(key >= rows, key - rows, key)
        row_pos = pos + lax.broadcasted_iota(jnp.int32, shape, 1) % rows
        return key_pos <= row_pos

    def scores(c, at, n):
        return dot(kd[c, pl.ds(at, n * keys)], q2, NT)

    def weighted(c, at, n, p):
        return dot(vt[c, :, pl.ds(at, n * keys)], p.astype(jnp.bfloat16), NN)

    def own_on(c):
        return (grp == 0) & (c * rows <= pos + rows - 1)

    @pl.when(fast[0] > 0)
    def _():
        for n in range(1, chips + 1):

            @pl.when(full_n == n)
            def _(n=n):
                for c in range(CHUNKS):
                    acc[...] = acc[...] + weighted(c, 0, n, jnp.exp2(scores(c, 0, n)))

        for c in range(CHUNKS):

            @pl.when(own_on(c))
            def _(c=c):
                p = jnp.where(admitted(c * rows), jnp.exp2(scores(c, chips * keys, 1)), 0.0)
                acc[...] = acc[...] + weighted(c, chips * keys, 1, p)

    @pl.when(fast[0] == 0)
    def _():
        def visit(c, at, s):
            old = m_ref[:1]
            new = jnp.maximum(old, jnp.max(s, axis=0, keepdims=True))
            acc[...] = acc[...] * jnp.exp2(old - new) + weighted(c, at, 1, jnp.exp2(s - new))
            m_ref[...] = jnp.broadcast_to(new, m_ref.shape)

        for c in range(CHUNKS):

            def body(chip, carry, c=c):
                at = pl.multiple_of(chip * keys, keys)
                visit(c, at, scores(c, at, 1))
                return carry

            lax.fori_loop(0, full_n, body, 0)

            @pl.when(own_on(c))
            def _(c=c):
                s = scores(c, chips * keys, 1)
                visit(c, chips * keys, jnp.where(admitted(c * rows), s, MASKED_SCORE))

    total = acc[width : width + 1]

    def write(merged):
        for h in range(heads):
            columns = slice(h * width, (h + 1) * width)
            value = merged[h * rows : (h + 1) * rows].astype(jnp.bfloat16)
            for sd in range(2):

                @pl.when(side == sd)
                def _(sd=sd, columns=columns, value=value):
                    outs[sd][:, columns] = value

    @pl.when(grp == 0)
    def _():
        write((acc[:width] * (1.0 / total)).T)

    @pl.when(grp == 1)
    def _():
        for i in range(2 * CHUNKS):

            @pl.when(blk == i)
            def _(i=i):
                part_ref[...] = parts[i][0]

        extra = part_ref[:, heads * width :].T
        lse_c = jnp.concatenate([extra[h : h + 1] for h in range(heads)], axis=1)
        flag = jnp.concatenate([extra[heads : heads + 1]] * heads, axis=1)
        o_c = jnp.concatenate(
            [part_ref[:, h * width : (h + 1) * width].T for h in range(heads)], axis=1
        )
        lse_p = jnp.where(flag > 0, m_ref[:1] + jnp.log2(total), MASKED_SCORE)
        top = jnp.maximum(lse_p, lse_c)
        w_p = jnp.exp2(lse_p - top)
        w_c = jnp.exp2(lse_c - top)
        rest = 1.0 / (w_p + w_c)
        write((acc[:width] * (w_p * rest / total) + o_c * (w_c * rest)).T)


def prompt_attention(heads, ids, norms, q, own, arrived, parts, rows_core, scale, after):
    slots_n = len(arrived[0])
    _, blocks, stacked, width = q.shape
    rows = stacked // heads
    keys = 2 * rows
    chips = slots_n // 2
    part_shape = (rows, heads * width + LANES)
    in_specs = [pl.BlockSpec(n.shape, lambda gi, blk, ids: (0, 0, 0)) for n in norms]
    in_specs += [pl.BlockSpec((1, 1, stacked, width), lambda gi, blk, ids: (gi, blk, 0, 0))]
    in_specs += [pl.BlockSpec((keys + PAD, 2 * width), lambda gi, blk, ids: (0, 0))] * (2 * CHUNKS)
    in_specs += [ANY] * (slots_n * CHUNKS)
    in_specs += [pl.BlockSpec((1,) + part_shape, lambda gi, blk, ids: (gi, 0, 0))] * len(parts)
    in_specs += [ANY] * len(after)
    out_block = (rows, heads * width)
    return call(
        functools.partial(prompt_kernel, heads, slots_n, rows_core, scale),
        "prompt_attention",
        (2, blocks),
        1,
        in_specs,
        [
            pl.BlockSpec(out_block, lambda gi, blk, ids: (blk // 2, 2 * ids[0] + gi)),
            pl.BlockSpec(out_block, lambda gi, blk, ids: (blk // 2, gi)),
        ],
        [
            jax.ShapeDtypeStruct((rows_core, 4 * heads * width), jnp.bfloat16),
            jax.ShapeDtypeStruct((rows_core, 2 * heads * width), jnp.bfloat16),
        ],
        [
            pltpu.VMEM((2, CHUNKS, chips, keys + PAD, 2 * width), jnp.bfloat16),
            pltpu.VMEM((CHUNKS, (chips + 1) * keys, 2 * width), jnp.bfloat16),
            pltpu.VMEM((CHUNKS, width + PAD, (chips + 1) * keys), jnp.bfloat16),
            pltpu.VMEM((width + PAD, stacked), jnp.float32),
            pltpu.VMEM((8, stacked), jnp.float32),
            pltpu.VMEM(part_shape, jnp.float32),
            pltpu.SMEM((1,), jnp.float32),
            pltpu.SemaphoreType.DMA((CHUNKS, slots_n)),
        ],
        cost=LARGE,
        mib=58,
    )(ids, *norms, q, *own[0], *own[1], *arrived[0], *arrived[1], *parts, *after)


def fill_kernel(ids, out_before, back, out):
    out[...] = back[...]


def fill_other_half(ids, out, back):
    rows, half = back.shape
    block = (rows // 2, half)
    return call(
        fill_kernel,
        "fill_other_half",
        (2,),
        1,
        [ANY, pl.BlockSpec(block, lambda i, ids: (i, 0))],
        pl.BlockSpec(block, lambda i, ids: (i, 1 - ids[0])),
        jax.ShapeDtypeStruct(out.shape, out.dtype),
        aliases={1: 0},
    )(ids, out, back)


def fast_shards(hidden, w_qkv, cache, cache_len, receive):
    head_width = cache.shape[3] // 2
    heads = w_qkv.shape[2] // head_width - 2
    rows_core = hidden.shape[1]
    rows = rows_core // CHUNKS
    draft = rows_core // cache.shape[0]
    scale = head_width ** (-0.5)
    seq_n = lax.axis_size("seq")
    chips = seq_n // 2
    ring_n = 2 * chips

    seq_i, group_i, mp_i = lax.axis_index("seq"), lax.axis_index("group"), lax.axis_index("mp")
    core = seq_i % 2
    ids = jnp.stack([core, seq_i // 2, group_i, mp_i]).astype(jnp.int32)

    mp_swap = [(0, 1), (1, 0)]
    core_swap = [(i, i ^ 1) for i in range(seq_n)]
    ring = [(0, k) for k in range(chips)] + [(1, chips - 1 - k) for k in range(chips)]
    index = [[g * seq_n + 2 * k + c for c in range(2)] for g, k in ring]
    up = [(index[r][c], index[(r + 1) % ring_n][c]) for r in range(ring_n) for c in range(2)]
    down = [(index[r][c], index[r - 1][c]) for r in range(ring_n) for c in range(2)]

    def swap_cores(x):
        return lax.ppermute(x, "seq", core_swap)

    def round_the_ring(block):
        ups, downs = [block], [block]
        for step in range(ring_n // 2):
            ups.append(lax.ppermute(ups[-1], ("group", "seq"), up))
            if step < ring_n // 2 - 1:
                downs.append(lax.ppermute(downs[-1], ("group", "seq"), down))
        return ups + downs[:0:-1]

    prefill = group_i == 0
    own = hidden[0]
    oth = [lax.ppermute(own[c * rows : (c + 1) * rows], "mp", mp_swap) for c in range(CHUNKS)]
    own_s = swap_cores(own)
    cache_t = jnp.transpose(cache, (2, 0, 1, 3))

    def cached(side, chunk, operands, after, span=None, before=None):
        common = (ids, cache_len, receive, cache_t, operands, chunk, rows, draft, scale, heads)
        return cache_attention(side, *common, after, LARGE, span, before)

    def projected(chunk, before, cost):
        return project(ids, own, own_s, oth[chunk], swap_cores(oth[chunk]), w_qkv, before, chunk, [], cost)

    oth[0] = after_all(oth[0], cache_t)
    q, theirs_0, kv_0, norms_0, kv0_0, kv1_0 = projected(0, None, SMALL)
    crossed_0 = lax.ppermute(kv1_0, "group", [(0, 1)])
    swapped_0 = swap_cores(theirs_0)
    oth[1] = after_all(oth[1], kv_0)

    q, theirs_1, kv_1, norms_1, kv0_1, kv1_1 = projected(1, q, LARGE)
    crossed_1 = lax.ppermute(kv1_1, "group", [(0, 1)])
    swapped_1 = swap_cores(theirs_1)
    ring_0 = round_the_ring(jnp.where(prefill, kv0_0, after_all(crossed_0, kv_1)))
    near_0 = cached(0, 0, (q, kv_0), [])
    ring_1 = round_the_ring(jnp.where(prefill, kv0_1, crossed_1))
    far_0 = cached(1, 0, (swapped_0,), [near_0])
    away_0 = swap_cores(far_0)
    far_1 = cached(1, 1, (swapped_1,), [far_0])
    away_1 = swap_cores(far_1)
    near_1 = cached(0, 1, (q, kv_1), [far_1])

    mine, theirs = prompt_attention(
        heads,
        ids,
        [norms_0, norms_1],
        q,
        [(kv0_0, kv1_0), (kv0_1, kv1_1)],
        [ring_0, ring_1],
        [near_0, away_0, near_1, away_1],
        rows_core,
        scale,
        [],
    )
    return fill_other_half(ids, mine, swap_cores(theirs))[None]


def plain_shards(hidden, w_qkv, cache, cache_len, receive):
    group_count = w_qkv.shape[0]
    column_count = w_qkv.shape[2]
    head_width = cache.shape[3] // 2
    heads_per_group = column_count // head_width - 2
    row_count = hidden.shape[1]
    requests = cache.shape[0]
    draft_count = row_count // requests
    slot_count = cache.shape[1]
    score_scale = head_width ** (-0.5)
    projected = jnp.einsum(
        "rd,gdc->grc",
        lax.all_gather(hidden, "mp", axis=2, tiled=True)[0],
        w_qkv,
        preferred_element_type=jnp.float32,
    ).astype(jnp.bfloat16)
    queries = projected[:, :, : heads_per_group * head_width].reshape(
        group_count, row_count, heads_per_group, head_width
    )
    new_kv = projected[:, :, heads_per_group * head_width :]
    prefill = lax.axis_index("group") == 0
    decode_on = jnp.logical_not(prefill)
    query_pos = lax.axis_index("seq") * row_count + jnp.arange(row_count, dtype=jnp.int32)
    admitted = jnp.repeat(receive, draft_count) > 0
    query_req = queries.reshape(group_count, requests, draft_count, heads_per_group, head_width)
    own_keys = new_kv[..., :head_width].reshape(group_count, requests, draft_count, head_width)
    own_values = new_kv[..., head_width:].reshape(group_count, requests, draft_count, head_width)
    cache_logits = (
        jnp.einsum(
            "gbtph,bugh->gbtpu",
            query_req,
            cache[..., :head_width],
            preferred_element_type=jnp.float32,
        )
        * score_scale
    )
    own_logits = (
        jnp.einsum("gbtph,gbuh->gbtpu", query_req, own_keys, preferred_element_type=jnp.float32)
        * score_scale
    )
    live_cache = (
        (jnp.arange(slot_count, dtype=jnp.int32)[None, :] < cache_len[:, None]) & decode_on
    )[None, :, None, None, :]
    causal = jnp.arange(draft_count)[None, :] <= jnp.arange(draft_count)[:, None]
    live_own = (causal & decode_on)[None, None, :, None, :]
    running_max = jnp.maximum(
        jnp.max(jnp.where(live_cache, cache_logits, MASKED_SCORE), axis=-1),
        jnp.max(jnp.where(live_own, own_logits, MASKED_SCORE), axis=-1),
    )
    cache_weights = jnp.where(live_cache, jnp.exp(cache_logits - running_max[..., None]), 0.0)
    own_weights = jnp.where(live_own, jnp.exp(own_logits - running_max[..., None]), 0.0)
    running_sum = jnp.sum(cache_weights, axis=-1) + jnp.sum(own_weights, axis=-1)
    weighted = jnp.einsum(
        "gbtpu,bugh->gbtph",
        cache_weights.astype(jnp.bfloat16),
        cache[..., head_width:],
        preferred_element_type=jnp.float32,
    )
    weighted = weighted + jnp.einsum(
        "gbtpu,gbuh->gbtph",
        own_weights.astype(jnp.bfloat16),
        own_values,
        preferred_element_type=jnp.float32,
    )
    carried_state = (
        running_max.reshape(group_count, row_count, heads_per_group),
        running_sum.reshape(group_count, row_count, heads_per_group),
        weighted.reshape(group_count, row_count, heads_per_group, head_width),
    )
    assembled = lax.all_gather(new_kv, "seq", axis=1, tiled=True)
    arrived = passed_along(assembled, "group", 1)
    prompt_kv = jnp.where(prefill, assembled, arrived)
    old_max, old_sum, old_weighted = carried_state
    key_count = prompt_kv.shape[1]
    logits = (
        jnp.einsum(
            "grph,gjh->grpj",
            queries,
            prompt_kv[..., :head_width],
            preferred_element_type=jnp.float32,
        )
        * score_scale
    )
    key_pos = jnp.arange(key_count, dtype=jnp.int32)
    allowed = jnp.where(prefill, key_pos[None, :] <= query_pos[:, None], admitted[:, None])[
        None, :, None, :
    ]
    new_max = jnp.maximum(old_max, jnp.max(jnp.where(allowed, logits, MASKED_SCORE), axis=-1))
    weights = jnp.where(allowed, jnp.exp(logits - new_max[..., None]), 0.0)
    rescale = jnp.exp(old_max - new_max)
    new_sum = old_sum * rescale + jnp.sum(weights, axis=-1)
    new_weighted = old_weighted * rescale[..., None] + jnp.einsum(
        "grpj,gjh->grph",
        weights.astype(jnp.bfloat16),
        prompt_kv[..., head_width:],
        preferred_element_type=jnp.float32,
    )
    carried_state = (new_max, new_sum, new_weighted)
    final_max, final_sum, final_weighted = carried_state
    output = (final_weighted / final_sum[..., None]).astype(jnp.bfloat16)
    return jnp.transpose(output, (1, 0, 2, 3)).reshape(
        1, row_count, group_count * heads_per_group * head_width
    )


def solution(mesh):
    def shards(hidden, w_qkv, cache, cache_len, receive):
        head_width = cache.shape[3] // 2
        fits = (
            mesh.shape["group"] == 2
            and mesh.shape["mp"] == 2
            and mesh.shape["seq"] % 2 == 0
            and w_qkv.shape[0] == 4
            and w_qkv.shape[2] == 6 * head_width
            and head_width == 128
            and hidden.shape[1] == CHUNKS * 8 * SUB_REQ * 4
            and hidden.shape[1] == 4 * cache.shape[0]
        )
        run = fast_shards if fits else plain_shards
        return run(hidden, w_qkv, cache, cache_len, receive)

    return jax.shard_map(
        shards,
        mesh=mesh,
        in_specs=(
            P("group", "seq", "mp"),
            P("mp", None, None),
            P("seq", None, "mp", None),
            P("seq"),
            P("seq"),
        ),
        out_specs=P("group", "seq", "mp"),
        check_vma=False,
    )
```

```python
import functools

import jax
import jax.numpy as jnp
from jax import lax
from jax.experimental import pallas as pl
from jax.experimental.pallas import tpu as pltpu
from jax.sharding import PartitionSpec as P

MASKED_SCORE = -1e30
SUB_REQ = 8
LANES = 128
CHUNKS = 2
PAD = 16
SAFE_LOGIT = 60.0
LOG2E = 1.4426950408889634
MIB = 1 << 20
NT = (((1,), (1,)), ((), ()))
NN = (((1,), (0,)), ((), ()))
ANY = pl.BlockSpec(memory_space=pltpu.HBM)
SMALL, LARGE = 1000, 200_000_000_000


def passed_along(block, axis, distance):
    devices = range(lax.axis_size(axis))
    route = [(i - distance, i) for i in devices if i - distance in devices]
    return lax.ppermute(block, axis, route)


def dot(a, b, dims):
    return lax.dot_general(a, b, dims, preferred_element_type=jnp.float32)


def call(kernel, name, grid, prefetch, in_specs, out_specs, out_shape, scratch=(), cost=SMALL, mib=48, aliases=None, free=()):
    made = pl.pallas_call(
        kernel,
        grid_spec=pltpu.PrefetchScalarGridSpec(
            num_scalar_prefetch=prefetch,
            grid=grid,
            in_specs=in_specs,
            out_specs=out_specs,
            scratch_shapes=list(scratch),
        ),
        out_shape=out_shape,
        input_output_aliases=aliases or {},
        compiler_params=pltpu.CompilerParams(
            dimension_semantics=("arbitrary",) * len(grid), vmem_limit_bytes=mib * MIB
        ),
        cost_estimate=pl.CostEstimate(flops=cost, bytes_accessed=SMALL, transcendentals=0),
        name=name,
    )

    def on(*args):
        kept = [
            x if i < prefetch or i in free else pltpu.with_memory_space_constraint(x, pltpu.HBM)
            for i, x in enumerate(args)
        ]
        return made(*kept)

    return on


def after_all(block, *before):
    return pl.pallas_call(
        lambda *refs: None,
        in_specs=[pl.BlockSpec(memory_space=pl.ANY)] * (1 + len(before)),
        out_specs=pl.BlockSpec(memory_space=pl.ANY),
        out_shape=jax.ShapeDtypeStruct(block.shape, block.dtype),
        input_output_aliases={0: 0},
        name="after_all",
    )(block, *before)


def take_kernel(ids, x, *refs):
    refs[-1][...] = x[...]


def take_rows(x, chunk, rows, after):
    block = (rows // 2, x.shape[1])
    return call(
        take_kernel,
        "take_rows",
        (2,),
        1,
        [pl.BlockSpec(block, lambda i, ids: (2 * chunk + i, 0))] + [ANY] * len(after),
        pl.BlockSpec(block, lambda i, ids: (i, 0)),
        jax.ShapeDtypeStruct((rows, x.shape[1]), x.dtype),
    )(jnp.zeros((1,), jnp.int32), x, *after)


def longest_row(x):
    wide = x.astype(jnp.float32)
    return jnp.max(jnp.sum(wide * wide, axis=1, keepdims=True), axis=0, keepdims=True)


def project_kernel(heads, ids, own, own_s, oth, oth_s, w, *refs):
    q_out, theirs, mine_kv, norms, kv0, kv1, total, top_rows = refs[-8:]
    gi, half = pl.program_id(0), pl.program_id(1)
    rows = own.shape[0]

    def product(mine, others):
        return dot(jnp.concatenate([mine[...], others[...]], axis=0), w[0], NN)

    @pl.when(half == 0)
    def _():
        total[...] = product(own, own_s)

    @pl.when(half == 1)
    def _():
        width = w.shape[2] // (heads + 2)
        longest = jnp.zeros((1, 1), jnp.float32)
        both = (total[...] + product(oth, oth_s)).astype(jnp.bfloat16)
        for side in range(2):
            here = slice(side * rows, (side + 1) * rows)
            res = both[here]
            for h in range(heads):
                q = res[:, h * width : (h + 1) * width]
                q_out[0, side, h * rows : (h + 1) * rows, :] = q
                longest = jnp.maximum(longest, longest_row(q))
            if side == 0:
                mine_kv[0] = res[:, heads * width :]
            else:
                theirs[0] = res

            def ring_form(out):
                k = res[:, heads * width : (heads + 1) * width]
                out[here, :width] = k
                for tile in range(rows // width):
                    lo = tile * width
                    out[side * rows + lo : side * rows + lo + width, width:] = res[
                        lo : lo + width, (heads + 1) * width :
                    ].T
                top = jnp.broadcast_to(longest_row(k) * 1.01, (PAD // 2, 2 * width))
                low = 2 * rows + side * (PAD // 2)
                top_rows[low - 2 * rows : low - 2 * rows + PAD // 2] = top

            @pl.when(gi == 0)
            def _():
                ring_form(kv0)

            @pl.when(gi == 1)
            def _():
                ring_form(kv1)

        norms[0] = jnp.broadcast_to(longest, norms.shape[1:])
        bound = top_rows[...].astype(jnp.bfloat16)

        @pl.when(gi == 0)
        def _():
            kv0[2 * rows :] = bound

        @pl.when(gi == 1)
        def _():
            kv1[2 * rows :] = bound


def project(ids, own, own_s, oth, oth_s, w, before, chunk, after, cost):
    rows, width = oth.shape
    columns = w.shape[2]
    kv_cols = columns // 3
    heads = 4
    head_width = kv_cols // 2

    x_specs = [pl.BlockSpec((rows, width), lambda i, half, ids: (chunk, 0))] * 2
    x_specs += [pl.BlockSpec((rows, width), lambda i, half, ids: (0, 0))] * 2
    in_specs = x_specs + [
        pl.BlockSpec((1, width, columns), lambda i, half, ids: (2 * ids[0] + i, half ^ ids[3], 0))
    ]
    args = [ids, own, own_s, oth, oth_s, w]
    aliases = {}
    if before is not None:
        aliases = {len(args): 0}
        in_specs.append(ANY)
        args.append(before)
    ring_shape = (2 * rows + PAD, kv_cols)
    whole = pl.BlockSpec(ring_shape, lambda i, half, ids: (0, 0))
    return call(
        functools.partial(project_kernel, heads),
        "project",
        (2, 2),
        1,
        in_specs + [ANY] * len(after),
        [
            pl.BlockSpec((1, 2, heads * rows, head_width), lambda i, half, ids: (i, chunk, 0, 0)),
            pl.BlockSpec((1, rows, columns), lambda i, half, ids: (i, 0, 0)),
            pl.BlockSpec((1, rows, kv_cols), lambda i, half, ids: (i, 0, 0)),
            pl.BlockSpec((1, 8, LANES), lambda i, half, ids: (i, 0, 0)),
            whole,
            whole,
        ],
        [
            jax.ShapeDtypeStruct((2, 2 * CHUNKS, heads * rows, head_width), jnp.bfloat16),
            jax.ShapeDtypeStruct((2, rows, columns), jnp.bfloat16),
            jax.ShapeDtypeStruct((2, rows, kv_cols), jnp.bfloat16),
            jax.ShapeDtypeStruct((2, 8, LANES), jnp.float32),
            jax.ShapeDtypeStruct(ring_shape, jnp.bfloat16),
            jax.ShapeDtypeStruct(ring_shape, jnp.bfloat16),
        ],
        [
            pltpu.VMEM((2 * rows, columns), jnp.float32),
            pltpu.VMEM((PAD, kv_cols), jnp.float32),
        ],
        cost=cost,
        mib=56,
        aliases=aliases,
        free=(2, 3, 4),
    )(*args, *after)


def cache_kernel(side, heads, draft, start_req, first_step, scale, ids, lens, receive, cache, *refs):
    out = refs[-1]
    _, step_req, slots, both = cache.shape
    width = both // 2
    rows = SUB_REQ * draft
    stacked = heads * rows
    step = pl.program_id(0) + first_step
    factor = scale * LOG2E

    @pl.when(ids[2] == 1)
    def _():
        row = lax.broadcasted_iota(jnp.int32, (stacked, slots), 0)
        req_of_row = row % rows // draft
        slot = lax.broadcasted_iota(jnp.int32, (stacked, slots), 1)
        own_row = lax.broadcasted_iota(jnp.int32, (stacked, rows), 0) % rows
        own_key = lax.broadcasted_iota(jnp.int32, (stacked, rows), 1)
        own_bias = jnp.where(
            (own_row // draft == own_key // draft) & (own_key <= own_row), 0.0, MASKED_SCORE
        )
        lane = lax.broadcasted_iota(jnp.int32, (rows, LANES), 1)
        req_of_lane_row = lax.broadcasted_iota(jnp.int32, (rows, LANES), 0) // draft
        chains, biases, flags = [], [], []
        for sub in range(step_req // SUB_REQ):
            req0 = start_req + step * step_req + sub * SUB_REQ
            biases.append(
                jnp.concatenate(
                    [
                        jnp.where((req_of_row == r) & (slot < lens[req0 + r]), 0.0, MASKED_SCORE)
                        for r in range(SUB_REQ)
                    ],
                    axis=1,
                )
            )
            flag = jnp.zeros((rows, LANES), jnp.float32)
            for r in range(SUB_REQ):
                flag = jnp.where(
                    (req_of_lane_row == r) & (receive[req0 + r] > 0) & (lane == heads), 1.0, flag
                )
            flags.append(flag)
            here = slice(sub * rows, (sub + 1) * rows)
            for gi in range(2):
                if side == 0:
                    q = refs[0]
                    per_head = q.shape[2] // heads
                    row0 = pl.multiple_of(step * (step_req * draft) + sub * rows, rows)
                    queries = [q[gi, 0, pl.ds(h * per_head + row0, rows), :] for h in range(heads)]
                    own = refs[1][gi, here, :]
                else:
                    block = refs[0][gi, here, :]
                    queries = [block[:, h * width : (h + 1) * width] for h in range(heads)]
                    own = block[:, heads * width :]
                kv = cache[gi, sub * SUB_REQ : (sub + 1) * SUB_REQ].reshape(SUB_REQ * slots, both)
                chains.append((gi, sub, here, jnp.concatenate(queries, axis=0), own, kv))
        s = [dot(q, kv[:, :width], NT) for _, _, _, q, own, kv in chains]
        s_own = [dot(q, own[:, :width], NT) for _, _, _, q, own, kv in chains]
        s = [x * factor + biases[chain[1]] for x, chain in zip(s, chains)]
        s_own = [x * factor + own_bias for x in s_own]
        top = [
            jnp.maximum(jnp.max(a, axis=1, keepdims=True), jnp.max(b, axis=1, keepdims=True))
            for a, b in zip(s, s_own)
        ]
        p = [jnp.exp2(x - t) for x, t in zip(s, top)]
        p_own = [jnp.exp2(x - t) for x, t in zip(s_own, top)]
        total = [
            jnp.sum(a, axis=1, keepdims=True) + jnp.sum(b, axis=1, keepdims=True)
            for a, b in zip(p, p_own)
        ]
        o = [
            dot(a.astype(jnp.bfloat16), kv[:, width:], NN)
            + dot(b.astype(jnp.bfloat16), own[:, width:], NN)
            for a, b, (_, _, _, _, own, kv) in zip(p, p_own, chains)
        ]
        for i, (gi, sub, here, _, _, _) in enumerate(chains):
            scaled = o[i] / total[i]
            lse = top[i] + jnp.log2(total[i])
            extra = flags[sub]
            for h in range(heads):
                part = slice(h * rows, (h + 1) * rows)
                out[gi, here, h * width : (h + 1) * width] = scaled[part]
                extra = jnp.where(lane == h, lse[part], extra)
            out[gi, here, heads * width :] = extra


def cache_attention(
    side, ids, lens, receive, cache_t, operands, chunk, rows, draft, scale, heads, after, cost, span=None, before=None
):
    _, _, slots, both = cache_t.shape
    width = both // 2
    step_req = 2 * SUB_REQ
    step_rows = step_req * draft
    steps = rows // step_rows
    lo, hi = span or (0, steps)
    first = chunk * steps + lo
    if side == 0:
        specs = [
            pl.BlockSpec(
                (2, 1, heads * rows, width), lambda i, ids, lens, receive: (0, 2 * chunk, 0, 0)
            )
        ]
        specs += [pl.BlockSpec((2, step_rows, both), lambda i, ids, lens, receive: (0, lo + i, 0))]
    else:
        columns = operands[0].shape[2]
        specs = [
            pl.BlockSpec((2, step_rows, columns), lambda i, ids, lens, receive: (0, lo + i, 0))
        ]

    aliases = {}
    if before is not None:
        aliases = {4 + len(operands) + len(after): 0}
        after = [*after, before]

    def cache_map(i, ids, lens, receive):
        return (ids[0] ^ side, (first + i) * ids[2], 0, 0)

    return call(
        functools.partial(cache_kernel, side, heads, draft, chunk * rows // draft, lo, scale),
        "cache_attention",
        (hi - lo,),
        3,
        [pl.BlockSpec((2, step_req, slots, both), cache_map)] + specs + [ANY] * len(after),
        pl.BlockSpec(
            (2, step_rows, heads * width + LANES), lambda i, ids, lens, receive: (0, lo + i, 0)
        ),
        jax.ShapeDtypeStruct((2, rows, heads * width + LANES), jnp.float32),
        cost=cost,
        aliases=aliases,
    )(ids, lens, receive, cache_t, *operands, *after)


def prompt_kernel(heads, slots_n, rows_core, scale, ids, *refs):
    refs = list(refs)
    norms = [refs.pop(0) for _ in range(CHUNKS)]
    q = refs.pop(0)
    own = [[refs.pop(0), refs.pop(0)] for _ in range(CHUNKS)]
    arrived = [[refs.pop(0) for _ in range(slots_n)] for _ in range(CHUNKS)]
    parts = [refs.pop(0) for _ in range(2 * CHUNKS)]
    outs = refs[-10:-8]
    kvbuf, kd, vt, acc, m_ref, part_ref, fast, sems = refs[-8:]
    gi, blk = pl.program_id(0), pl.program_id(1)
    core, z, grp = ids[0], ids[1], ids[2]
    chips = slots_n // 2
    place = jnp.where(grp == 0, z, slots_n - 1 - z)
    keys = kvbuf.shape[3] - PAD
    stacked, width = q.shape[2:]
    rows = stacked // heads

    def each(act):
        for c in range(CHUNKS):
            for t in range(slots_n):
                r = lax.rem(place - t + slots_n, slots_n)
                chip = jnp.where(r < chips, r, slots_n - 1 - r)
                lane = jnp.where(r < chips, 0, 1)
                act(pltpu.make_async_copy(arrived[c][t], kvbuf.at[lane, c, chip], sems.at[c, t]))

    def place_block(c, at, block):
        k = block[:keys, :width]
        kd[c, at * keys : (at + 1) * keys, :width] = k
        kd[c, at * keys : (at + 1) * keys, width:] = k
        for lo in range(0, keys, width):
            vt[c, :width, at * keys + lo : at * keys + lo + width] = block[lo : lo + width, width:]
        return block[keys:, :].astype(jnp.float32)

    @pl.when((gi == 0) & (blk == 0))
    def _():
        each(lambda copy: copy.start())
        row = lax.broadcasted_iota(jnp.int32, (PAD, vt.shape[2]), 0)
        for c in range(CHUNKS):
            vt[c, width:, :] = jnp.where(row == 0, 1.0, 0.0).astype(jnp.bfloat16)
        each(lambda copy: copy.wait())

    @pl.when(blk == 0)
    def _():
        longest = jnp.zeros((PAD, 2 * width), jnp.float32)
        for c in range(CHUNKS):
            for at in range(chips):
                longest = jnp.maximum(longest, place_block(c, at, kvbuf.at[gi, c, at]))
            for g in range(2):

                @pl.when(gi == g)
                def _(c=c, g=g):
                    part_ref[:PAD, : 2 * width] = place_block(c, chips, own[c][g])

            longest = jnp.maximum(longest, part_ref[:PAD, : 2 * width])
        top_q = norms[0][...]
        for other in norms[1:]:
            top_q = jnp.maximum(top_q, other[...])
        fast[0] = jnp.where(
            jnp.max(longest) * jnp.max(top_q) * (1.02 * scale * scale)
            <= SAFE_LOGIT * SAFE_LOGIT,
            1.0,
            0.0,
        )

    acc[...] = jnp.zeros_like(acc)
    m_ref[...] = jnp.where(fast[0] > 0, 0.0, jnp.full_like(m_ref, MASKED_SCORE))

    wide = q[0, 0].astype(jnp.float32) * (scale * LOG2E)
    high = wide.astype(jnp.bfloat16)
    low = (wide - high.astype(jnp.float32)).astype(jnp.bfloat16)
    q2 = jnp.concatenate([high, low], axis=1)

    side = blk % 2
    pos = (core ^ side) * rows_core + blk // 2 * rows
    full_n = jnp.where(grp == 0, z, chips)

    def admitted(key_start):
        shape = (keys, stacked)
        key = lax.broadcasted_iota(jnp.int32, shape, 0)
        key_core = jnp.where(key >= rows, 1 - core, core)
        key_pos = key_start + key_core * rows_core + jnp.where(key >= rows, key - rows, key)
        row_pos = pos + lax.broadcasted_iota(jnp.int32, shape, 1) % rows
        return key_pos <= row_pos

    def scores(c, at, n):
        return dot(kd[c, pl.ds(at, n * keys)], q2, NT)

    def weighted(c, at, n, p):
        return dot(vt[c, :, pl.ds(at, n * keys)], p.astype(jnp.bfloat16), NN)

    def own_on(c):
        return (grp == 0) & (c * rows <= pos + rows - 1)

    @pl.when(fast[0] > 0)
    def _():
        for n in range(1, chips + 1):

            @pl.when(full_n == n)
            def _(n=n):
                for c in range(CHUNKS):
                    acc[...] = acc[...] + weighted(c, 0, n, jnp.exp2(scores(c, 0, n)))

        for c in range(CHUNKS):

            @pl.when(own_on(c))
            def _(c=c):
                p = jnp.where(admitted(c * rows), jnp.exp2(scores(c, chips * keys, 1)), 0.0)
                acc[...] = acc[...] + weighted(c, chips * keys, 1, p)

    @pl.when(fast[0] == 0)
    def _():
        def visit(c, at, s):
            old = m_ref[:1]
            new = jnp.maximum(old, jnp.max(s, axis=0, keepdims=True))
            acc[...] = acc[...] * jnp.exp2(old - new) + weighted(c, at, 1, jnp.exp2(s - new))
            m_ref[...] = jnp.broadcast_to(new, m_ref.shape)

        for c in range(CHUNKS):

            def body(chip, carry, c=c):
                at = pl.multiple_of(chip * keys, keys)
                visit(c, at, scores(c, at, 1))
                return carry

            lax.fori_loop(0, full_n, body, 0)

            @pl.when(own_on(c))
            def _(c=c):
                s = scores(c, chips * keys, 1)
                visit(c, chips * keys, jnp.where(admitted(c * rows), s, MASKED_SCORE))

    total = acc[width : width + 1]

    def write(merged):
        for h in range(heads):
            columns = slice(h * width, (h + 1) * width)
            value = merged[h * rows : (h + 1) * rows].astype(jnp.bfloat16)
            for sd in range(2):

                @pl.when(side == sd)
                def _(sd=sd, columns=columns, value=value):
                    outs[sd][:, columns] = value

    @pl.when(grp == 0)
    def _():
        write((acc[:width] * (1.0 / total)).T)

    @pl.when(grp == 1)
    def _():
        for i in range(2 * CHUNKS):

            @pl.when(blk == i)
            def _(i=i):
                part_ref[...] = parts[i][0]

        extra = part_ref[:, heads * width :].T
        lse_c = jnp.concatenate([extra[h : h + 1] for h in range(heads)], axis=1)
        flag = jnp.concatenate([extra[heads : heads + 1]] * heads, axis=1)
        o_c = jnp.concatenate(
            [part_ref[:, h * width : (h + 1) * width].T for h in range(heads)], axis=1
        )
        lse_p = jnp.where(flag > 0, m_ref[:1] + jnp.log2(total), MASKED_SCORE)
        top = jnp.maximum(lse_p, lse_c)
        w_p = jnp.exp2(lse_p - top)
        w_c = jnp.exp2(lse_c - top)
        rest = 1.0 / (w_p + w_c)
        write((acc[:width] * (w_p * rest / total) + o_c * (w_c * rest)).T)


def prompt_attention(heads, ids, norms, q, own, arrived, parts, rows_core, scale, after):
    slots_n = len(arrived[0])
    _, blocks, stacked, width = q.shape
    rows = stacked // heads
    keys = 2 * rows
    chips = slots_n // 2
    part_shape = (rows, heads * width + LANES)
    in_specs = [pl.BlockSpec(n.shape, lambda gi, blk, ids: (0, 0, 0)) for n in norms]
    in_specs += [pl.BlockSpec((1, 1, stacked, width), lambda gi, blk, ids: (gi, blk, 0, 0))]
    in_specs += [pl.BlockSpec((keys + PAD, 2 * width), lambda gi, blk, ids: (0, 0))] * (2 * CHUNKS)
    in_specs += [ANY] * (slots_n * CHUNKS)
    in_specs += [pl.BlockSpec((1,) + part_shape, lambda gi, blk, ids: (gi, 0, 0))] * len(parts)
    in_specs += [ANY] * len(after)
    out_block = (rows, heads * width)
    return call(
        functools.partial(prompt_kernel, heads, slots_n, rows_core, scale),
        "prompt_attention",
        (2, blocks),
        1,
        in_specs,
        [
            pl.BlockSpec(out_block, lambda gi, blk, ids: (blk // 2, 2 * ids[0] + gi)),
            pl.BlockSpec(out_block, lambda gi, blk, ids: (blk // 2, gi)),
        ],
        [
            jax.ShapeDtypeStruct((rows_core, 4 * heads * width), jnp.bfloat16),
            jax.ShapeDtypeStruct((rows_core, 2 * heads * width), jnp.bfloat16),
        ],
        [
            pltpu.VMEM((2, CHUNKS, chips, keys + PAD, 2 * width), jnp.bfloat16),
            pltpu.VMEM((CHUNKS, (chips + 1) * keys, 2 * width), jnp.bfloat16),
            pltpu.VMEM((CHUNKS, width + PAD, (chips + 1) * keys), jnp.bfloat16),
            pltpu.VMEM((width + PAD, stacked), jnp.float32),
            pltpu.VMEM((8, stacked), jnp.float32),
            pltpu.VMEM(part_shape, jnp.float32),
            pltpu.SMEM((1,), jnp.float32),
            pltpu.SemaphoreType.DMA((CHUNKS, slots_n)),
        ],
        cost=LARGE,
        mib=58,
        free=range(2 + 3 * CHUNKS + slots_n * CHUNKS, 2 + 3 * CHUNKS + slots_n * CHUNKS + len(parts)),
    )(ids, *norms, q, *own[0], *own[1], *arrived[0], *arrived[1], *parts, *after)


def fill_kernel(ids, out_before, back, out):
    out[...] = back[...]


def fill_other_half(ids, out, back):
    rows, half = back.shape
    block = (rows // 2, half)
    return call(
        fill_kernel,
        "fill_other_half",
        (2,),
        1,
        [ANY, pl.BlockSpec(block, lambda i, ids: (i, 0))],
        pl.BlockSpec(block, lambda i, ids: (i, 1 - ids[0])),
        jax.ShapeDtypeStruct(out.shape, out.dtype),
        aliases={1: 0},
        free=(2,),
    )(ids, out, back)


def fast_shards(hidden, w_qkv, cache, cache_len, receive):
    head_width = cache.shape[3] // 2
    heads = w_qkv.shape[2] // head_width - 2
    rows_core = hidden.shape[1]
    rows = rows_core // CHUNKS
    draft = rows_core // cache.shape[0]
    scale = head_width ** (-0.5)
    seq_n = lax.axis_size("seq")
    chips = seq_n // 2
    ring_n = 2 * chips

    seq_i, group_i, mp_i = lax.axis_index("seq"), lax.axis_index("group"), lax.axis_index("mp")
    core = seq_i % 2
    ids = jnp.stack([core, seq_i // 2, group_i, mp_i]).astype(jnp.int32)

    mp_swap = [(0, 1), (1, 0)]
    core_swap = [(i, i ^ 1) for i in range(seq_n)]
    ring = [(0, k) for k in range(chips)] + [(1, chips - 1 - k) for k in range(chips)]
    index = [[g * seq_n + 2 * k + c for c in range(2)] for g, k in ring]
    up = [(index[r][c], index[(r + 1) % ring_n][c]) for r in range(ring_n) for c in range(2)]
    down = [(index[r][c], index[r - 1][c]) for r in range(ring_n) for c in range(2)]

    def swap_cores(x):
        return lax.ppermute(x, "seq", core_swap)

    def round_the_ring(block):
        ups, downs = [block], [block]
        for step in range(ring_n // 2):
            ups.append(lax.ppermute(ups[-1], ("group", "seq"), up))
            if step < ring_n // 2 - 1:
                downs.append(lax.ppermute(downs[-1], ("group", "seq"), down))
        return ups + downs[:0:-1]

    prefill = group_i == 0
    own = hidden[0]
    pieces = []
    for c in range(CHUNKS):
        pieces.append(take_rows(own, c, rows, pieces[-1:]))
    oth = [lax.ppermute(piece, "mp", mp_swap) for piece in pieces]
    own_s = swap_cores(own)
    cache_t = jnp.transpose(cache, (2, 0, 1, 3))

    def cached(side, chunk, operands, after, span=None, before=None):
        common = (ids, cache_len, receive, cache_t, operands, chunk, rows, draft, scale, heads)
        return cache_attention(side, *common, after, LARGE, span, before)

    def projected(chunk, before, cost):
        return project(ids, own, own_s, oth[chunk], swap_cores(oth[chunk]), w_qkv, before, chunk, [], cost)

    oth[0] = after_all(oth[0], cache_t)
    q, theirs_0, kv_0, norms_0, kv0_0, kv1_0 = projected(0, None, SMALL)
    crossed_0 = lax.ppermute(kv1_0, "group", [(0, 1)])
    swapped_0 = swap_cores(theirs_0)
    near_0 = cached(0, 0, (q, kv_0), [])
    oth[1] = after_all(oth[1], near_0)

    q, theirs_1, kv_1, norms_1, kv0_1, kv1_1 = projected(1, q, LARGE)
    crossed_1 = lax.ppermute(kv1_1, "group", [(0, 1)])
    swapped_1 = swap_cores(theirs_1)
    ring_0 = round_the_ring(jnp.where(prefill, kv0_0, after_all(crossed_0, kv_1)))
    ring_1 = round_the_ring(jnp.where(prefill, kv0_1, crossed_1))
    far_0 = cached(1, 0, (swapped_0,), [near_0])
    away_0 = swap_cores(far_0)
    far_1 = cached(1, 1, (swapped_1,), [far_0])
    away_1 = swap_cores(far_1)
    near_1 = cached(0, 1, (q, kv_1), [far_1])

    mine, theirs = prompt_attention(
        heads,
        ids,
        [norms_0, norms_1],
        q,
        [(kv0_0, kv1_0), (kv0_1, kv1_1)],
        [ring_0, ring_1],
        [near_0, away_0, near_1, away_1],
        rows_core,
        scale,
        [],
    )
    return fill_other_half(ids, mine, swap_cores(theirs))[None]


def plain_shards(hidden, w_qkv, cache, cache_len, receive):
    group_count = w_qkv.shape[0]
    column_count = w_qkv.shape[2]
    head_width = cache.shape[3] // 2
    heads_per_group = column_count // head_width - 2
    row_count = hidden.shape[1]
    requests = cache.shape[0]
    draft_count = row_count // requests
    slot_count = cache.shape[1]
    score_scale = head_width ** (-0.5)
    projected = jnp.einsum(
        "rd,gdc->grc",
        lax.all_gather(hidden, "mp", axis=2, tiled=True)[0],
        w_qkv,
        preferred_element_type=jnp.float32,
    ).astype(jnp.bfloat16)
    queries = projected[:, :, : heads_per_group * head_width].reshape(
        group_count, row_count, heads_per_group, head_width
    )
    new_kv = projected[:, :, heads_per_group * head_width :]
    prefill = lax.axis_index("group") == 0
    decode_on = jnp.logical_not(prefill)
    query_pos = lax.axis_index("seq") * row_count + jnp.arange(row_count, dtype=jnp.int32)
    admitted = jnp.repeat(receive, draft_count) > 0
    query_req = queries.reshape(group_count, requests, draft_count, heads_per_group, head_width)
    own_keys = new_kv[..., :head_width].reshape(group_count, requests, draft_count, head_width)
    own_values = new_kv[..., head_width:].reshape(group_count, requests, draft_count, head_width)
    cache_logits = (
        jnp.einsum(
            "gbtph,bugh->gbtpu",
            query_req,
            cache[..., :head_width],
            preferred_element_type=jnp.float32,
        )
        * score_scale
    )
    own_logits = (
        jnp.einsum("gbtph,gbuh->gbtpu", query_req, own_keys, preferred_element_type=jnp.float32)
        * score_scale
    )
    live_cache = (
        (jnp.arange(slot_count, dtype=jnp.int32)[None, :] < cache_len[:, None]) & decode_on
    )[None, :, None, None, :]
    causal = jnp.arange(draft_count)[None, :] <= jnp.arange(draft_count)[:, None]
    live_own = (causal & decode_on)[None, None, :, None, :]
    running_max = jnp.maximum(
        jnp.max(jnp.where(live_cache, cache_logits, MASKED_SCORE), axis=-1),
        jnp.max(jnp.where(live_own, own_logits, MASKED_SCORE), axis=-1),
    )
    cache_weights = jnp.where(live_cache, jnp.exp(cache_logits - running_max[..., None]), 0.0)
    own_weights = jnp.where(live_own, jnp.exp(own_logits - running_max[..., None]), 0.0)
    running_sum = jnp.sum(cache_weights, axis=-1) + jnp.sum(own_weights, axis=-1)
    weighted = jnp.einsum(
        "gbtpu,bugh->gbtph",
        cache_weights.astype(jnp.bfloat16),
        cache[..., head_width:],
        preferred_element_type=jnp.float32,
    )
    weighted = weighted + jnp.einsum(
        "gbtpu,gbuh->gbtph",
        own_weights.astype(jnp.bfloat16),
        own_values,
        preferred_element_type=jnp.float32,
    )
    carried_state = (
        running_max.reshape(group_count, row_count, heads_per_group),
        running_sum.reshape(group_count, row_count, heads_per_group),
        weighted.reshape(group_count, row_count, heads_per_group, head_width),
    )
    assembled = lax.all_gather(new_kv, "seq", axis=1, tiled=True)
    arrived = passed_along(assembled, "group", 1)
    prompt_kv = jnp.where(prefill, assembled, arrived)
    old_max, old_sum, old_weighted = carried_state
    key_count = prompt_kv.shape[1]
    logits = (
        jnp.einsum(
            "grph,gjh->grpj",
            queries,
            prompt_kv[..., :head_width],
            preferred_element_type=jnp.float32,
        )
        * score_scale
    )
    key_pos = jnp.arange(key_count, dtype=jnp.int32)
    allowed = jnp.where(prefill, key_pos[None, :] <= query_pos[:, None], admitted[:, None])[
        None, :, None, :
    ]
    new_max = jnp.maximum(old_max, jnp.max(jnp.where(allowed, logits, MASKED_SCORE), axis=-1))
    weights = jnp.where(allowed, jnp.exp(logits - new_max[..., None]), 0.0)
    rescale = jnp.exp(old_max - new_max)
    new_sum = old_sum * rescale + jnp.sum(weights, axis=-1)
    new_weighted = old_weighted * rescale[..., None] + jnp.einsum(
        "grpj,gjh->grph",
        weights.astype(jnp.bfloat16),
        prompt_kv[..., head_width:],
        preferred_element_type=jnp.float32,
    )
    carried_state = (new_max, new_sum, new_weighted)
    final_max, final_sum, final_weighted = carried_state
    output = (final_weighted / final_sum[..., None]).astype(jnp.bfloat16)
    return jnp.transpose(output, (1, 0, 2, 3)).reshape(
        1, row_count, group_count * heads_per_group * head_width
    )


def solution(mesh):
    def shards(hidden, w_qkv, cache, cache_len, receive):
        head_width = cache.shape[3] // 2
        fits = (
            mesh.shape["group"] == 2
            and mesh.shape["mp"] == 2
            and mesh.shape["seq"] % 2 == 0
            and w_qkv.shape[0] == 4
            and w_qkv.shape[2] == 6 * head_width
            and head_width == 128
            and hidden.shape[1] == CHUNKS * 8 * SUB_REQ * 4
            and hidden.shape[1] == 4 * cache.shape[0]
        )
        run = fast_shards if fits else plain_shards
        return run(hidden, w_qkv, cache, cache_len, receive)

    return jax.shard_map(
        shards,
        mesh=mesh,
        in_specs=(
            P("group", "seq", "mp"),
            P("mp", None, None),
            P("seq", None, "mp", None),
            P("seq"),
            P("seq"),
        ),
        out_specs=P("group", "seq", "mp"),
        check_vma=False,
    )
```
